32 devices in a mesh: row: 4 (over y, core), col: 2 (over x), rep: 4 (over z).
Axes of the slice: x: 2, y: 2, z: 4, core: 2. Of those that a mesh axis runs over, the one named last changes fastest.
Arguments:
- a_weights: bfloat16 [4, 4096, 512], P('rep', 'row', 'col'), may hold values from 0 to 10000, as said below
- a_flags: int32 [4, 32, 4], P('rep', 'row', 'col'), may hold values 0 or 1
- b_weights: bfloat16 [4, 512, 4096], P('rep', 'row', 'col'), may hold values from 0 to 10000, as said below
- b_flags: int32 [4, 4, 32], P('rep', 'row', 'col'), may hold values 0 or 1
- out_flags: int32 [32, 32], P('row', ('col', 'rep')), may hold values 0 or 1
Outputs:
- two_hop: bfloat16 [4096, 4096], P('row', ('col', 'rep'))
The draws below stay inside these ranges and needn't reach their ends.
Inputs may be any that keep to these rules, and one draw needn't show every extreme that they name: `a_weights`: positive edge weights. `b_weights`: positive edge weights.
All inputs are finite; a program needn't handle non-finite values. No bound on the sum of `a_flags` or of `b_flags` or of `out_flags` on one device may be relied on, other than what follows from the above.
Results may differ from the reference program's by a relative error of at most 0.012.
Values may be sent and summed in bfloat16 or wider, within the bound.
A program may use at most 64 MiB of HBM per device.

```python
import math
import jax
import jax.numpy as jnp
from jax import lax

TILE = 128
MB = 32
KG = 4
KW = 4
NB = 32


def heavy_weights(key, groups, rows, cols):
    first, second, third = jax.random.split(key, 3)
    normal_part = jnp.clip(jax.random.normal(first, (groups, rows, cols), jnp.float32), -3.5, 3.5)
    base = jnp.exp(1.2 * normal_part)
    col_scale = jnp.exp(math.log(10.0) * jax.random.uniform(second, (groups, 1, cols), jnp.float32))
    row_scale = jnp.exp(math.log(4.0) * jax.random.uniform(third, (groups, rows, 1), jnp.float32))
    ramp = 1.0 + 2.0 * jnp.arange(cols, dtype=jnp.float32) / cols
    return (base * col_scale * row_scale * ramp[None, None, :]).astype(jnp.bfloat16)


def draw_a_weights(key, part):
    return heavy_weights(jax.random.fold_in(key, 11), KG, MB * TILE, KW * TILE)


def draw_b_weights(key, part):
    return heavy_weights(jax.random.fold_in(key, 23), KG, KW * TILE, NB * TILE)


def with_ends(entries, stream_key, low, top_value):
    extent = entries.shape
    spot = [jax.random.randint(jax.random.fold_in(stream_key, axis), (), 0, extent[axis]) for axis in range(len(extent))]
    entries = entries.at[tuple(spot)].set(low)
    longest = extent.index(max(extent))
    spot[longest] = (spot[longest] + 1) % extent[longest]
    return entries.at[tuple(spot)].set(top_value)


def setup_inputs(seed: int = 0) -> dict:
    key_of = jax.random.split(jax.random.key(seed), 6)
    a_weights = draw_a_weights(jax.random.fold_in(key_of[5], 71), 0)
    a_flags = with_ends((jax.random.randint(key_of[1], (KG, MB, KW), 0, 2) < 1).astype(jnp.int32), jax.random.fold_in(key_of[1], 1), 0, 1)
    b_weights = draw_b_weights(jax.random.fold_in(key_of[5], 71), 0)
    b_flags = with_ends((jax.random.randint(key_of[3], (KG, KW, NB), 0, 2) < 1).astype(jnp.int32), jax.random.fold_in(key_of[3], 1), 0, 1)
    out_flags = with_ends((jax.random.randint(key_of[4], (MB, NB), 0, 3) < 2).astype(jnp.int32), jax.random.fold_in(key_of[4], 1), 0, 1)
    return dict(a_weights=a_weights, a_flags=a_flags, b_weights=b_weights, b_flags=b_flags, out_flags=out_flags)


def expand(flags):
    return jnp.repeat(jnp.repeat(flags, TILE, axis=-2), TILE, axis=-1)


def reference(a_weights, a_flags, b_weights, b_flags, out_flags):
    a_masked = a_weights * expand(a_flags).astype(jnp.bfloat16)
    deg_a = 1.0 + jnp.sum(a_masked.astype(jnp.float32), axis=(0, 2))
    walk_a = (a_masked.astype(jnp.float32) / deg_a[None, :, None]).astype(jnp.bfloat16)
    total = jnp.zeros((MB * TILE, NB * TILE), jnp.float32)
    for group in range(KG):
        b_masked = b_weights[group] * expand(b_flags[group]).astype(jnp.bfloat16)
        deg_b = 1.0 + jnp.sum(b_masked.astype(jnp.float32), axis=1)
        walk_b = (b_masked.astype(jnp.float32) / deg_b[:, None]).astype(jnp.bfloat16)
        group_part = jnp.dot(walk_a[group], walk_b, preferred_element_type=jnp.float32).astype(jnp.bfloat16)
        group_part = lax.optimization_barrier(group_part)
        total = total + group_part.astype(jnp.float32)
    factor = jnp.float32(NB * TILE)
    return (factor * total * expand(out_flags).astype(jnp.float32)).astype(jnp.bfloat16)
```

```python
import functools

import jax
import jax.numpy as jnp
from jax import lax
from jax.experimental import pallas as pl
from jax.experimental.pallas import tpu as pltpu
from jax.sharding import PartitionSpec as P

MESH = pl.DeviceIdType.MESH


def kernel(
    n_r, n_c, n_p, nch, factor,
    af, bf, of, a, b, out,
    abuf, bm, bsl, bbuf, dego, degr, acc, dacc,
    zr, zsl, zsr, xr, xs, bzr, bzs, byr, bys, dr, ds,
):
    r, c, p = lax.axis_index("row"), lax.axis_index("col"), lax.axis_index("rep")
    rows, ka = a.shape
    kb = b.shape[0]
    width = rows // af.shape[0]
    cols = out.shape[1]
    ch_rows = rows // nch

    barrier = pltpu.get_barrier_semaphore()
    for axis, mine, count in (("row", r, n_r), ("col", c, n_c), ("rep", p, n_p)):
        for o in range(1, count):
            pl.semaphore_signal(
                barrier, inc=1, device_id={axis: lax.rem(mine + o, count)}, device_id_type=MESH
            )

    for i in range(bf.shape[0]):
        for j in range(bf.shape[1]):
            at = (slice(i * width, (i + 1) * width), slice(j * width, (j + 1) * width))
            bm[at] = (b[at].astype(jnp.float32) * bf[i, j].astype(jnp.float32)).astype(jnp.bfloat16)
    dego[...] = jnp.dot(
        bm[...], jnp.ones((bm.shape[1], 128), jnp.bfloat16), preferred_element_type=jnp.float32
    )
    for i in range(af.shape[0]):
        ch, off = divmod(i * width, ch_rows)
        for j in range(af.shape[1]):
            tile = a[i * width:(i + 1) * width, j * width:(j + 1) * width].astype(jnp.float32)
            abuf[p, c, ch, off:off + width, j * width:(j + 1) * width] = (
                tile * af[i, j].astype(jnp.float32)
            ).astype(jnp.bfloat16)

    pl.semaphore_wait(barrier, n_r + n_c + n_p - 3)

    def deg_copy(cc):
        return pltpu.make_async_remote_copy(
            src_ref=dego, dst_ref=degr.at[c], send_sem=ds.at[cc], recv_sem=dr.at[c],
            device_id={"col": cc}, device_id_type=MESH)

    def z_copy(g, ch, to, send):
        block = abuf.at[g, c, ch]
        return pltpu.make_async_remote_copy(
            src_ref=block, dst_ref=block, send_sem=send.at[g, ch], recv_sem=zr.at[g, ch],
            device_id={"rep": to}, device_id_type=MESH)

    def x_copy(g, ch, cc):
        block = abuf.at[g, c, ch]
        return pltpu.make_async_remote_copy(
            src_ref=block, dst_ref=block, send_sem=xs.at[g, cc, ch], recv_sem=xr.at[g, c, ch],
            device_id={"col": cc}, device_id_type=MESH)

    def bz_copy(pp):
        return pltpu.make_async_remote_copy(
            src_ref=bsl.at[pp], dst_ref=bbuf.at[p, pl.ds(pl.multiple_of(r * kb, kb), kb)],
            send_sem=bzs.at[pp], recv_sem=bzr.at[p], device_id={"rep": pp}, device_id_type=MESH)

    def by_copy(g, rr):
        block = bbuf.at[g, pl.ds(pl.multiple_of(r * kb, kb), kb)]
        return pltpu.make_async_remote_copy(
            src_ref=block, dst_ref=block, send_sem=bys.at[g, rr], recv_sem=byr.at[g, r],
            device_id={"row": rr}, device_id_type=MESH)

    def arrived(ref, sem):
        pltpu.make_async_copy(ref, ref, sem).wait()

    def others(mine, count, f):
        @pl.loop(1, count)
        def _(o):
            f(lax.rem(mine + o, count))

    def forward(g, ch):
        others(c, n_c, lambda cc: x_copy(g, ch, cc).start())

    others(c, n_c, lambda cc: deg_copy(cc).start())

    @pl.loop(0, nch)
    def _(ch):
        @pl.when(p > 0)
        def _():
            z_copy(p, ch, p - 1, zsl).start()

        @pl.when(p < n_p - 1)
        def _():
            z_copy(p, ch, p + 1, zsr).start()

        forward(p, ch)

    def add_deg(cc):
        arrived(degr.at[cc], dr.at[cc])
        dego_sum[...] += degr[cc]

    dego_sum = dacc.at[pl.ds(0, kb)]
    dego_sum[...] = 1.0 + dego[...]
    others(c, n_c, add_deg)
    for t in range(bm.shape[1] // 128):
        pp, off = divmod(t * 128, cols)
        bsl[pp, :, off:off + 128] = (
            bm[:, t * 128:(t + 1) * 128].astype(jnp.float32) / dego_sum[...]
        ).astype(jnp.bfloat16)
    others(p, n_p, lambda pp: bz_copy(pp).start())
    bbuf[p, pl.ds(pl.multiple_of(r * kb, kb), kb)] = bsl[p]
    others(r, n_r, lambda rr: by_copy(p, rr).start())

    for d in range(1, n_p):
        @pl.loop(0, nch)
        def _(ch):
            @pl.when(p >= d)
            def _():
                g = p - d
                arrived(abuf.at[g, c, ch], zr.at[g, ch])

                @pl.when(p < n_p - 1)
                def _():
                    z_copy(g, ch, p + 1, zsr).start()

                forward(g, ch)

            @pl.when(p + d < n_p)
            def _():
                g = p + d
                arrived(abuf.at[g, c, ch], zr.at[g, ch])

                @pl.when(p > 0)
                def _():
                    z_copy(g, ch, p - 1, zsl).start()

                forward(g, ch)

        def pass_b(g):
            arrived(bbuf.at[g, pl.ds(pl.multiple_of(r * kb, kb), kb)], bzr.at[g])
            others(r, n_r, lambda rr: by_copy(g, rr).start())

        @pl.when(p >= d)
        def _():
            pass_b(p - d)

        @pl.when(p + d < n_p)
        def _():
            pass_b(p + d)

    acc[...] = jnp.zeros_like(acc)
    dacc[...] = jnp.ones_like(dacc)

    def block(g, cc, ch):
        left = abuf[g, cc, ch]
        right = bbuf[g, pl.ds(pl.multiple_of(cc * ka, ka), ka)]
        at = pl.ds(pl.multiple_of(ch * ch_rows, ch_rows), ch_rows)
        acc[at] += jnp.dot(left, right, preferred_element_type=jnp.float32)
        dacc[at] += jnp.dot(
            left, jnp.ones((ka, 128), jnp.bfloat16), preferred_element_type=jnp.float32
        )

    def by_side(f):
        for d in range(n_p):
            @pl.when(p >= d)
            def _():
                f(p - d)

            if d:
                @pl.when(p + d < n_p)
                def _():
                    f(p + d)

    def own(g):
        def wait_b(rr):
            arrived(bbuf.at[g, pl.ds(pl.multiple_of(rr * kb, kb), kb)], byr.at[g, rr])

        others(r, n_r, wait_b)

        @pl.loop(0, nch)
        def _(ch):
            block(g, c, ch)

    by_side(own)

    def crossed(g):
        def one(cc):
            @pl.loop(0, nch)
            def _(ch):
                arrived(abuf.at[g, cc, ch], xr.at[g, cc, ch])
                block(g, cc, ch)

        others(c, n_c, one)

    by_side(crossed)

    @pl.loop(0, of.shape[0])
    def _(i):
        at = pl.ds(pl.multiple_of(i * width, width), width)
        scale = factor / dacc[at]
        for j in range(of.shape[1]):
            tile = slice(j * width, (j + 1) * width)
            out[at, tile] = (
                acc[at, tile] * (scale * of[i, j].astype(jnp.float32))
            ).astype(jnp.bfloat16)

    others(c, n_c, lambda cc: deg_copy(cc).wait_send())
    others(p, n_p, lambda pp: bz_copy(pp).wait_send())

    @pl.loop(0, n_p)
    def _(g):
        others(r, n_r, lambda rr: by_copy(g, rr).wait_send())

        @pl.loop(0, nch)
        def _(ch):
            others(c, n_c, lambda cc: x_copy(g, ch, cc).wait_send())

            @pl.when((g >= p) & (p > 0))
            def _():
                z_copy(g, ch, p - 1, zsl).wait_send()

            @pl.when((g <= p) & (p < n_p - 1))
            def _():
                z_copy(g, ch, p + 1, zsr).wait_send()


def shards(a_weights, a_flags, b_weights, b_flags, out_flags):
    n_r, n_c, n_p = (lax.axis_size(axis) for axis in ("row", "col", "rep"))
    _, rows, ka = a_weights.shape
    _, kb, wide = b_weights.shape
    cols = wide // n_p
    nch = max(1, 8 // n_c)
    dma = pltpu.SemaphoreType.DMA
    smem = pl.BlockSpec(memory_space=pltpu.SMEM)
    vmem = pl.BlockSpec(memory_space=pltpu.VMEM)
    return pl.pallas_call(
        functools.partial(kernel, n_r, n_c, n_p, nch, float(wide * n_c)),
        out_shape=jax.ShapeDtypeStruct((rows, cols), jnp.bfloat16),
        in_specs=[smem] * 3 + [vmem] * 2,
        out_specs=vmem,
        scratch_shapes=[
            pltpu.VMEM((n_p, n_c, nch, rows // nch, ka), jnp.bfloat16),
            pltpu.VMEM((kb, wide), jnp.bfloat16),
            pltpu.VMEM((n_p, kb, cols), jnp.bfloat16),
            pltpu.VMEM((n_p, n_r * kb, cols), jnp.bfloat16),
            pltpu.VMEM((kb, 128), jnp.float32),
            pltpu.VMEM((n_c, kb, 128), jnp.float32),
            pltpu.VMEM((rows, cols), jnp.float32),
            pltpu.VMEM((rows, 128), jnp.float32),
            dma((n_p, nch)), dma((n_p, nch)), dma((n_p, nch)),
            dma((n_p, n_c, nch)), dma((n_p, n_c, nch)),
            dma((n_p,)), dma((n_p,)),
            dma((n_p, n_r)), dma((n_p, n_r)),
            dma((n_c,)), dma((n_c,)),
        ],
        compiler_params=pltpu.CompilerParams(
            collective_id=0, has_side_effects=True, vmem_limit_bytes=56 * 2**20
        ),
    )(a_flags[0], b_flags[0], out_flags, a_weights[0], b_weights[0])


def solution(mesh):
    return jax.shard_map(
        shards,
        mesh=mesh,
        in_specs=(
            P("rep", "row", "col"),
            P("rep", "row", "col"),
            P("rep", "row", "col"),
            P("rep", "row", "col"),
            P("row", ("col", "rep")),
        ),
        out_specs=P("row", ("col", "rep")),
        check_vma=False,
    )
```

```python
import functools

import jax
import jax.numpy as jnp
from jax import lax
from jax.experimental import pallas as pl
from jax.experimental.pallas import tpu as pltpu
from jax.sharding import PartitionSpec as P

MESH = pl.DeviceIdType.MESH


def kernel(
    n_r, n_c, n_p, nch, factor,
    af, bf, of, a, b, out,
    abuf, bm, bsl, bbuf, dego, degr, acc, dacc,
    zr, zsl, zsr, xr, xs, bzr, bzs, byr, bys, dr, ds,
):
    r, c, p = lax.axis_index("row"), lax.axis_index("col"), lax.axis_index("rep")
    rows, ka = a.shape
    kb = b.shape[0]
    width = rows // af.shape[0]
    cols = out.shape[1]
    ch_rows = rows // nch

    barrier = pltpu.get_barrier_semaphore()
    for axis, mine, count in (("row", r, n_r), ("col", c, n_c), ("rep", p, n_p)):
        for o in range(1, count):
            pl.semaphore_signal(
                barrier, inc=1, device_id={axis: lax.rem(mine + o, count)}, device_id_type=MESH
            )

    for i in range(bf.shape[0]):
        for j in range(bf.shape[1]):
            at = (slice(i * width, (i + 1) * width), slice(j * width, (j + 1) * width))
            bm[at] = (b[at].astype(jnp.float32) * bf[i, j].astype(jnp.float32)).astype(jnp.bfloat16)
    dego[...] = jnp.dot(
        bm[...], jnp.ones((bm.shape[1], 128), jnp.bfloat16), preferred_element_type=jnp.float32
    )
    for i in range(af.shape[0]):
        ch, off = divmod(i * width, ch_rows)
        for j in range(af.shape[1]):
            tile = a[i * width:(i + 1) * width, j * width:(j + 1) * width].astype(jnp.float32)
            abuf[p, c, ch, off:off + width, j * width:(j + 1) * width] = (
                tile * af[i, j].astype(jnp.float32)
            ).astype(jnp.bfloat16)

    pl.semaphore_wait(barrier, n_r + n_c + n_p - 3)

    def deg_copy(cc):
        return pltpu.make_async_remote_copy(
            src_ref=dego, dst_ref=degr.at[c], send_sem=ds.at[cc], recv_sem=dr.at[c],
            device_id={"col": cc}, device_id_type=MESH)

    def z_copy(g, ch, to, send):
        block = abuf.at[g, c, ch]
        return pltpu.make_async_remote_copy(
            src_ref=block, dst_ref=block, send_sem=send.at[g, ch], recv_sem=zr.at[g, ch],
            device_id={"rep": to}, device_id_type=MESH)

    def x_copy(g, ch, cc):
        block = abuf.at[g, c, ch]
        return pltpu.make_async_remote_copy(
            src_ref=block, dst_ref=block, send_sem=xs.at[g, cc, ch], recv_sem=xr.at[g, c, ch],
            device_id={"col": cc}, device_id_type=MESH)

    def bz_copy(pp):
        return pltpu.make_async_remote_copy(
            src_ref=bsl.at[pp], dst_ref=bbuf.at[p, pl.ds(pl.multiple_of(r * kb, kb), kb)],
            send_sem=bzs.at[pp], recv_sem=bzr.at[p], device_id={"rep": pp}, device_id_type=MESH)

    def by_copy(g, rr):
        block = bbuf.at[g, pl.ds(pl.multiple_of(r * kb, kb), kb)]
        return pltpu.make_async_remote_copy(
            src_ref=block, dst_ref=block, send_sem=bys.at[g, rr], recv_sem=byr.at[g, r],
            device_id={"row": rr}, device_id_type=MESH)

    def arrived(ref, sem):
        pltpu.make_async_copy(ref, ref, sem).wait()

    def others(mine, count, f):
        @pl.loop(1, count)
        def _(o):
            f(lax.rem(mine + o, count))

    def forward(g, ch):
        others(c, n_c, lambda cc: x_copy(g, ch, cc).start())

    others(c, n_c, lambda cc: deg_copy(cc).start())

    @pl.loop(0, nch)
    def _(ch):
        @pl.when(p > 0)
        def _():
            z_copy(p, ch, p - 1, zsl).start()

        @pl.when(p < n_p - 1)
        def _():
            z_copy(p, ch, p + 1, zsr).start()

        forward(p, ch)

    def add_deg(cc):
        arrived(degr.at[cc], dr.at[cc])
        dego_sum[...] += degr[cc]

    dego_sum = dacc.at[pl.ds(0, kb)]
    dego_sum[...] = 1.0 + dego[...]
    others(c, n_c, add_deg)
    for t in range(bm.shape[1] // 128):
        pp, off = divmod(t * 128, cols)
        bsl[pp, :, off:off + 128] = (
            bm[:, t * 128:(t + 1) * 128].astype(jnp.float32) / dego_sum[...]
        ).astype(jnp.bfloat16)
    others(p, n_p, lambda pp: bz_copy(pp).start())
    bbuf[p, pl.ds(pl.multiple_of(r * kb, kb), kb)] = bsl[p]
    others(r, n_r, lambda rr: by_copy(p, rr).start())

    acc[...] = jnp.zeros_like(acc)
    dacc[...] = jnp.ones_like(dacc)

    def by_side(d, f):
        @pl.when(p >= d)
        def _():
            f(p - d)

        if d:
            @pl.when(p + d < n_p)
            def _():
                f(p + d)

    def block(g, cc, ch):
        left = abuf[g, cc, ch]
        right = bbuf[g, pl.ds(pl.multiple_of(cc * ka, ka), ka)]
        at = pl.ds(pl.multiple_of(ch * ch_rows, ch_rows), ch_rows)
        acc[at] += jnp.dot(left, right, preferred_element_type=jnp.float32)
        dacc[at] += jnp.dot(
            left, jnp.ones((ka, 128), jnp.bfloat16), preferred_element_type=jnp.float32
        )

    def own(d, ch):
        def one(g):
            @pl.when(ch == 0)
            def _():
                others(r, n_r, lambda rr: arrived(
                    bbuf.at[g, pl.ds(pl.multiple_of(rr * kb, kb), kb)], byr.at[g, rr]))

            block(g, c, ch)

        by_side(d, one)

    def crossed(d, ch):
        def one(g):
            def from_col(cc):
                arrived(abuf.at[g, cc, ch], xr.at[g, cc, ch])
                block(g, cc, ch)

            others(c, n_c, from_col)

        by_side(d, one)

    for d in range(1, n_p + 2):
        @pl.loop(0, nch)
        def _(ch):
            def pass_a(g):
                arrived(abuf.at[g, c, ch], zr.at[g, ch])

                @pl.when((g < p) & (p < n_p - 1))
                def _():
                    z_copy(g, ch, p + 1, zsr).start()

                @pl.when((g > p) & (p > 0))
                def _():
                    z_copy(g, ch, p - 1, zsl).start()

                forward(g, ch)

            if d < n_p:
                by_side(d, pass_a)
            if d <= n_p:
                own(d - 1, ch)
            if d >= 2:
                crossed(d - 2, ch)

        def pass_b(g):
            arrived(bbuf.at[g, pl.ds(pl.multiple_of(r * kb, kb), kb)], bzr.at[g])
            others(r, n_r, lambda rr: by_copy(g, rr).start())

        if d < n_p:
            by_side(d, pass_b)

    @pl.loop(0, of.shape[0])
    def _(i):
        at = pl.ds(pl.multiple_of(i * width, width), width)
        scale = factor / dacc[at]
        for j in range(of.shape[1]):
            tile = slice(j * width, (j + 1) * width)
            out[at, tile] = (
                acc[at, tile] * (scale * of[i, j].astype(jnp.float32))
            ).astype(jnp.bfloat16)

    others(c, n_c, lambda cc: deg_copy(cc).wait_send())
    others(p, n_p, lambda pp: bz_copy(pp).wait_send())

    @pl.loop(0, n_p)
    def _(g):
        others(r, n_r, lambda rr: by_copy(g, rr).wait_send())

        @pl.loop(0, nch)
        def _(ch):
            others(c, n_c, lambda cc: x_copy(g, ch, cc).wait_send())

            @pl.when((g >= p) & (p > 0))
            def _():
                z_copy(g, ch, p - 1, zsl).wait_send()

            @pl.when((g <= p) & (p < n_p - 1))
            def _():
                z_copy(g, ch, p + 1, zsr).wait_send()


def shards(a_weights, a_flags, b_weights, b_flags, out_flags):
    n_r, n_c, n_p = (lax.axis_size(axis) for axis in ("row", "col", "rep"))
    _, rows, ka = a_weights.shape
    _, kb, wide = b_weights.shape
    cols = wide // n_p
    nch = max(1, 8 // n_c)
    dma = pltpu.SemaphoreType.DMA
    smem = pl.BlockSpec(memory_space=pltpu.SMEM)
    vmem = pl.BlockSpec(memory_space=pltpu.VMEM)
    return pl.pallas_call(
        functools.partial(kernel, n_r, n_c, n_p, nch, float(wide * n_c)),
        out_shape=jax.ShapeDtypeStruct((rows, cols), jnp.bfloat16),
        in_specs=[smem] * 3 + [vmem] * 2,
        out_specs=vmem,
        scratch_shapes=[
            pltpu.VMEM((n_p, n_c, nch, rows // nch, ka), jnp.bfloat16),
            pltpu.VMEM((kb, wide), jnp.bfloat16),
            pltpu.VMEM((n_p, kb, cols), jnp.bfloat16),
            pltpu.VMEM((n_p, n_r * kb, cols), jnp.bfloat16),
            pltpu.VMEM((kb, 128), jnp.float32),
            pltpu.VMEM((n_c, kb, 128), jnp.float32),
            pltpu.VMEM((rows, cols), jnp.float32),
            pltpu.VMEM((rows, 128), jnp.float32),
            dma((n_p, nch)), dma((n_p, nch)), dma((n_p, nch)),
            dma((n_p, n_c, nch)), dma((n_p, n_c, nch)),
            dma((n_p,)), dma((n_p,)),
            dma((n_p, n_r)), dma((n_p, n_r)),
            dma((n_c,)), dma((n_c,)),
        ],
        compiler_params=pltpu.CompilerParams(
            collective_id=0, has_side_effects=True, vmem_limit_bytes=56 * 2**20
        ),
    )(a_flags[0], b_flags[0], out_flags, a_weights[0], b_weights[0])


def solution(mesh):
    return jax.shard_map(
        shards,
        mesh=mesh,
        in_specs=(
            P("rep", "row", "col"),
            P("rep", "row", "col"),
            P("rep", "row", "col"),
            P("rep", "row", "col"),
            P("row", ("col", "rep")),
        ),
        out_specs=P("row", ("col", "rep")),
        check_vma=False,
    )
```

```python
import functools

import jax
import jax.numpy as jnp
from jax import lax
from jax.experimental import pallas as pl
from jax.experimental.pallas import tpu as pltpu
from jax.sharding import PartitionSpec as P

MESH = pl.DeviceIdType.MESH


def kernel(
    n_r, n_c, n_p, nch, factor,
    af, bf, of, a, b, out,
    abuf, bm, bsl, bbuf, dego, degr, acc, dacc, obuf, oin,
    zr, zsl, zsr, xr, xs, ts, bzr, bzs, bes, byr, bys, dr, ds, orecv, osend,
):
    r, c, p = lax.axis_index("row"), lax.axis_index("col"), lax.axis_index("rep")
    rows, ka = a.shape
    kb = b.shape[0]
    width = rows // af.shape[0]
    cols = out.shape[1]
    ch_rows = rows // nch
    per_ch = ch_rows // width
    half = nch // 2
    last = n_p - 1
    is_end = (p == 0) | (p == last)
    is_mid = (p > 0) & (p < last)
    upper = lax.div(p, n_p // 2)
    end = upper * last
    helper = 1 + upper * (last - 2)

    barrier = pltpu.get_barrier_semaphore()
    for axis, mine, count in (("row", r, n_r), ("col", c, n_c), ("rep", p, n_p)):
        for o in range(1, count):
            pl.semaphore_signal(
                barrier, inc=1, device_id={axis: lax.rem(mine + o, count)}, device_id_type=MESH
            )

    for i in range(bf.shape[0]):
        for j in range(bf.shape[1]):
            at = (slice(i * width, (i + 1) * width), slice(j * width, (j + 1) * width))
            bm[at] = (b[at].astype(jnp.float32) * bf[i, j].astype(jnp.float32)).astype(jnp.bfloat16)
    dego[...] = jnp.dot(
        bm[...], jnp.ones((bm.shape[1], 128), jnp.bfloat16), preferred_element_type=jnp.float32
    )
    for i in range(af.shape[0]):
        ch, off = divmod(i * width, ch_rows)
        for j in range(af.shape[1]):
            tile = a[i * width:(i + 1) * width, j * width:(j + 1) * width].astype(jnp.float32)
            abuf[p, c, ch, off:off + width, j * width:(j + 1) * width] = (
                tile * af[i, j].astype(jnp.float32)
            ).astype(jnp.bfloat16)

    pl.semaphore_wait(barrier, n_r + n_c + n_p - 3)

    def remote(src, dst, send, recv, **to):
        return pltpu.make_async_remote_copy(
            src_ref=src, dst_ref=dst, send_sem=send, recv_sem=recv,
            device_id=to, device_id_type=MESH)

    def arrived(ref, sem):
        pltpu.make_async_copy(ref, ref, sem).wait()

    def others(mine, count, f):
        @pl.loop(1, count)
        def _(o):
            f(lax.rem(mine + o, count))

    def start(copy):
        copy.start()

    def wait_send(copy):
        copy.wait_send()

    def z_copies(g, ch, act):
        block = abuf.at[g, c, ch]

        @pl.when((g >= p) & (p > 0) & ((p > 1) | (ch >= half)))
        def _():
            act(remote(block, block, zsl.at[g, ch], zr.at[g, ch], rep=p - 1))

        @pl.when((g <= p) & (p < last) & ((p < last - 1) | (ch >= half)))
        def _():
            act(remote(block, block, zsr.at[g, ch], zr.at[g, ch], rep=p + 1))

    def x_copies(g, ch, act):
        block = abuf.at[g, c, ch]

        @pl.when((g == p) | (is_mid & (g != end)) | (is_end & (ch >= half)))
        def _():
            others(c, n_c, lambda cc: act(
                remote(block, block, xs.at[g, cc, ch], xr.at[g, c, ch], col=cc)))

    def turn_copies(ch, act, wait):
        def one(cc):
            block = abuf.at[p, cc, ch]
            if wait:
                arrived(block, xr.at[p, cc, ch])
            act(remote(block, block, ts.at[cc, ch], xr.at[p, cc, ch], rep=helper))

        others(c, n_c, one)

    def b_rows(slot, g, rr):
        return bbuf.at[slot, g, pl.ds(pl.multiple_of(rr * kb, kb), kb)]

    def bz_copies(act):
        for pp, ee in ((1, 0), (last - 1, last)):
            @pl.when(p != pp)
            def _():
                for slot, part in ((0, pp), (1, ee)):
                    act(remote(
                        bsl.at[part], b_rows(slot, p, r), bzs.at[slot, pp], bzr.at[slot, p], rep=pp))

    def be_copy(g):
        return remote(b_rows(1, g, r), b_rows(0, g, r), bes.at[g], bzr.at[0, g], rep=end)

    def flip(index, bit):
        return index + bit - 2 * bit * lax.rem(lax.div(index, bit), 2)

    steps = []
    held = [()]
    bit = n_r // 2
    while bit:
        steps.append((bit, list(held)))
        held += [flips + (bit,) for flips in held]
        bit //= 2

    def flipped(flips):
        index = r
        for bit in flips:
            index = flip(index, bit)
        return index

    def by_copies(slot, g, step, act):
        bit, blocks = steps[step]
        for flips in blocks:
            rr = flipped(flips)
            block = b_rows(slot, g, rr)
            act(remote(block, block, bys.at[slot, g, step, rr], byr.at[slot, g, rr], row=flip(r, bit)))

    def by_arrived(slot, g, step):
        bit, blocks = steps[step]
        for flips in blocks:
            rr = flipped(flips + (bit,))
            arrived(b_rows(slot, g, rr), byr.at[slot, g, rr])

    def each_slot(f):
        f(0)

        @pl.when(is_mid)
        def _():
            f(1)

    def pass_b(g):
        def one(slot):
            @pl.when(g != p)
            def _():
                arrived(b_rows(slot, g, r), bzr.at[slot, g])

            by_copies(slot, g, 0, start)
            if slot == 1:
                @pl.when(g != end)
                def _():
                    be_copy(g).start()

        each_slot(one)

    def relay_b(g):
        def one(slot):
            for step in range(1, len(steps)):
                by_arrived(slot, g, step - 1)
                by_copies(slot, g, step, start)

        each_slot(one)

    def by_side(d, f):
        @pl.when(p >= d)
        def _():
            f(p - d)

        @pl.when(p + d < n_p)
        def _():
            f(p + d)

    def pass_a(d, low, high):
        @pl.loop(low, high)
        def _(ch):
            def one(g):
                arrived(abuf.at[g, c, ch], zr.at[g, ch])
                z_copies(g, ch, start)
                x_copies(g, ch, start)

            by_side(d, one)

    def send_own(low, high):
        @pl.loop(low, high)
        def _(ch):
            z_copies(p, ch, start)
            x_copies(p, ch, start)

    def deg_copy(cc):
        return remote(dego, degr.at[c], ds.at[cc], dr.at[c], col=cc)

    others(c, n_c, lambda cc: deg_copy(cc).start())
    send_own(0, half)

    deg = dacc.at[pl.ds(0, kb)]
    deg[...] = 1.0 + dego[...]

    def add_deg(cc):
        arrived(degr.at[cc], dr.at[cc])
        deg[...] += degr[cc]

    others(c, n_c, add_deg)
    for t in range(bm.shape[1] // 128):
        pp, off = divmod(t * 128, cols)
        bsl[pp, :, off:off + 128] = (
            bm[:, t * 128:(t + 1) * 128].astype(jnp.float32) / deg[...]
        ).astype(jnp.bfloat16)
    bz_copies(start)
    mine = pl.ds(pl.multiple_of(r * kb, kb), kb)
    bbuf[0, p, mine] = bsl[p]

    @pl.when(is_mid)
    def _():
        bbuf[1, p, mine] = bsl[end]

    pass_b(p)
    send_own(half, nch)

    def chunk(ch, slots):
        acc[...] = jnp.zeros_like(acc)
        dacc[...] = jnp.ones_like(dacc)
        top = dacc.at[pl.ds(0, ch_rows)]
        for g in range(n_p):
            def one(cc):
                left = abuf[g, cc, ch]
                for slot in range(slots):
                    right = bbuf[slot, g, pl.ds(pl.multiple_of(cc * ka, ka), ka)]
                    acc[slot] += jnp.dot(left, right, preferred_element_type=jnp.float32)
                top[...] += jnp.dot(
                    left, jnp.ones((ka, 128), jnp.bfloat16), preferred_element_type=jnp.float32
                )

            def from_col(cc):
                @pl.when(is_mid | (p != g))
                def _():
                    arrived(abuf.at[g, cc, ch], xr.at[g, cc, ch])

                one(cc)

            one(c)
            others(c, n_c, from_col)
        for i in range(per_ch):
            part = slice(i * width, (i + 1) * width)
            scale = factor / dacc[part]
            at = pl.ds(pl.multiple_of(ch * ch_rows + i * width, width), width)
            for j in range(of.shape[1]):
                tile = slice(j * width, (j + 1) * width)
                flag = of[ch * per_ch + i, j].astype(jnp.float32)
                out[at, tile] = (acc[0, part, tile] * (scale * flag)).astype(jnp.bfloat16)
                if slots == 2:
                    obuf[ch, part, tile] = (acc[1, part, tile] * scale).astype(jnp.bfloat16)

    def o_copy(ch):
        return remote(obuf.at[ch], oin.at[ch], osend.at[ch], orecv.at[ch], rep=end)

    def done_b():
        for g in range(n_p):
            each_slot(lambda slot: by_arrived(slot, g, len(steps) - 1))

    @pl.when(is_end)
    def _():
        def turn(low, high):
            @pl.loop(low, high)
            def _(ch):
                turn_copies(ch, start, True)

        turn(0, half)
        relay_b(p)
        turn(half, nch)
        for d in range(1, n_p):
            by_side(d, pass_b)
            pass_a(d, half, nch)
            by_side(d, relay_b)

    @pl.when(is_mid)
    def _():
        pass_a(1, 0, half)
        relay_b(p)
        by_side(1, pass_b)
        for d in range(2, n_p - 1):
            pass_a(d, 0, half)
            by_side(d - 1, relay_b)
            by_side(d, pass_b)
        pass_a(1, half, nch)
        by_side(n_p - 2, relay_b)

    done_b()

    @pl.when(is_mid)
    def _():
        @pl.loop(0, half)
        def _(ch):
            chunk(ch, 2)
            o_copy(ch).start()

        for d in range(2, n_p - 1):
            pass_a(d, half, nch)

    @pl.loop(half, nch)
    def _(ch):
        chunk(ch, 1)

    @pl.when(is_end)
    def _():
        @pl.loop(0, half)
        def _(ch):
            arrived(oin.at[ch], orecv.at[ch])
            for i in range(per_ch):
                at = pl.ds(pl.multiple_of(ch * ch_rows + i * width, width), width)
                for j in range(of.shape[1]):
                    tile = slice(j * width, (j + 1) * width)
                    flag = of[ch * per_ch + i, j].astype(jnp.float32)
                    part = oin[ch, i * width:(i + 1) * width, tile].astype(jnp.float32)
                    out[at, tile] = (part * flag).astype(jnp.bfloat16)

    others(c, n_c, lambda cc: deg_copy(cc).wait_send())
    bz_copies(wait_send)

    @pl.loop(0, n_p)
    def _(g):
        def sent(slot):
            for step in range(len(steps)):
                by_copies(slot, g, step, wait_send)
            if slot == 1:
                @pl.when(g != end)
                def _():
                    be_copy(g).wait_send()

        each_slot(sent)

        @pl.loop(0, nch)
        def _(ch):
            @pl.when((g == p) | is_mid | (ch >= half))
            def _():
                z_copies(g, ch, wait_send)
                x_copies(g, ch, wait_send)

    @pl.when(is_end)
    def _():
        @pl.loop(0, nch)
        def _(ch):
            turn_copies(ch, wait_send, False)

    @pl.when(is_mid)
    def _():
        @pl.loop(0, half)
        def _(ch):
            o_copy(ch).wait_send()


def shards(a_weights, a_flags, b_weights, b_flags, out_flags):
    n_r, n_c, n_p = (lax.axis_size(axis) for axis in ("row", "col", "rep"))
    _, rows, ka = a_weights.shape
    _, kb, wide = b_weights.shape
    cols = wide // n_p
    nch = max(2, 16 // n_c)
    dma = pltpu.SemaphoreType.DMA
    smem = pl.BlockSpec(memory_space=pltpu.SMEM)
    vmem = pl.BlockSpec(memory_space=pltpu.VMEM)
    return pl.pallas_call(
        functools.partial(kernel, n_r, n_c, n_p, nch, float(wide * n_c)),
        out_shape=jax.ShapeDtypeStruct((rows, cols), jnp.bfloat16),
        in_specs=[smem] * 3 + [vmem] * 2,
        out_specs=vmem,
        scratch_shapes=[
            pltpu.VMEM((n_p, n_c, nch, rows // nch, ka), jnp.bfloat16),
            pltpu.VMEM((kb, wide), jnp.bfloat16),
            pltpu.VMEM((n_p, kb, cols), jnp.bfloat16),
            pltpu.VMEM((2, n_p, n_r * kb, cols), jnp.bfloat16),
            pltpu.VMEM((kb, 128), jnp.float32),
            pltpu.VMEM((n_c, kb, 128), jnp.float32),
            pltpu.VMEM((2, rows // nch, cols), jnp.float32),
            pltpu.VMEM((max(kb, rows // nch), 128), jnp.float32),
            pltpu.VMEM((nch // 2, rows // nch, cols), jnp.bfloat16),
            pltpu.VMEM((nch // 2, rows // nch, cols), jnp.bfloat16),
            dma((n_p, nch)), dma((n_p, nch)), dma((n_p, nch)),
            dma((n_p, n_c, nch)), dma((n_p, n_c, nch)), dma((n_c, nch)),
            dma((2, n_p)), dma((2, n_p)), dma((n_p,)),
            dma((2, n_p, n_r)), dma((2, n_p, n_r.bit_length(), n_r)),
            dma((n_c,)), dma((n_c,)),
            dma((nch // 2,)), dma((nch // 2,)),
        ],
        compiler_params=pltpu.CompilerParams(
            collective_id=0, has_side_effects=True, vmem_limit_bytes=56 * 2**20
        ),
    )(a_flags[0], b_flags[0], out_flags, a_weights[0], b_weights[0])


def solution(mesh):
    return jax.shard_map(
        shards,
        mesh=mesh,
        in_specs=(
            P("rep", "row", "col"),
            P("rep", "row", "col"),
            P("rep", "row", "col"),
            P("rep", "row", "col"),
            P("row", ("col", "rep")),
        ),
        out_specs=P("row", ("col", "rep")),
        check_vma=False,
    )
```

```python
import functools

import jax
import jax.numpy as jnp
from jax import lax
from jax.experimental import pallas as pl
from jax.experimental.pallas import tpu as pltpu
from jax.sharding import PartitionSpec as P

MESH = pl.DeviceIdType.MESH


def kernel(
    n_r, n_c, n_p, nch, factor,
    af, bf, of, a, b, out,
    abuf, bm, bsl, bbuf, dego, degr, acc, dacc, obuf, oin,
    zr, zsl, zsr, xr, xs, ts, bzr, bzs, bes, byr, bys, dr, ds, orecv, osend,
):
    r, c, p = lax.axis_index("row"), lax.axis_index("col"), lax.axis_index("rep")
    rows, ka = a.shape
    kb = b.shape[0]
    width = rows // af.shape[0]
    cols = out.shape[1]
    ch_rows = rows // nch
    per_ch = ch_rows // width
    half = obuf.shape[0]
    last = n_p - 1
    is_end = (p == 0) | (p == last)
    is_mid = (p > 0) & (p < last)
    upper = lax.div(p, n_p // 2)
    end = upper * last
    helper = 1 + upper * (last - 2)

    barrier = pltpu.get_barrier_semaphore()
    for axis, mine, count in (("row", r, n_r), ("col", c, n_c), ("rep", p, n_p)):
        for o in range(1, count):
            pl.semaphore_signal(
                barrier, inc=1, device_id={axis: lax.rem(mine + o, count)}, device_id_type=MESH
            )

    for i in range(bf.shape[0]):
        for j in range(bf.shape[1]):
            at = (slice(i * width, (i + 1) * width), slice(j * width, (j + 1) * width))
            bm[at] = (b[at].astype(jnp.float32) * bf[i, j].astype(jnp.float32)).astype(jnp.bfloat16)
    dego[...] = jnp.dot(
        bm[...], jnp.ones((bm.shape[1], 128), jnp.bfloat16), preferred_element_type=jnp.float32
    )
    for i in range(af.shape[0]):
        ch, off = divmod(i * width, ch_rows)
        for j in range(af.shape[1]):
            tile = a[i * width:(i + 1) * width, j * width:(j + 1) * width].astype(jnp.float32)
            abuf[p, c, ch, off:off + width, j * width:(j + 1) * width] = (
                tile * af[i, j].astype(jnp.float32)
            ).astype(jnp.bfloat16)

    pl.semaphore_wait(barrier, n_r + n_c + n_p - 3)

    def remote(src, dst, send, recv, **to):
        return pltpu.make_async_remote_copy(
            src_ref=src, dst_ref=dst, send_sem=send, recv_sem=recv,
            device_id=to, device_id_type=MESH)

    def arrived(ref, sem):
        pltpu.make_async_copy(ref, ref, sem).wait()

    def others(mine, count, f):
        @pl.loop(1, count)
        def _(o):
            f(lax.rem(mine + o, count))

    def start(copy):
        copy.start()

    def wait_send(copy):
        copy.wait_send()

    def z_copies(g, ch, act):
        block = abuf.at[g, c, ch]

        @pl.when((g >= p) & (p > 0) & ((p > 1) | (ch >= half)))
        def _():
            act(remote(block, block, zsl.at[g, ch], zr.at[g, ch], rep=p - 1))

        @pl.when((g <= p) & (p < last) & ((p < last - 1) | (ch >= half)))
        def _():
            act(remote(block, block, zsr.at[g, ch], zr.at[g, ch], rep=p + 1))

    def x_copies(g, ch, act):
        block = abuf.at[g, c, ch]

        @pl.when((g == p) | (is_mid & (g != end)) | (is_end & (ch >= half)))
        def _():
            others(c, n_c, lambda cc: act(
                remote(block, block, xs.at[g, cc, ch], xr.at[g, c, ch], col=cc)))

    def turn_copies(ch, act, wait):
        def one(cc):
            block = abuf.at[p, cc, ch]
            if wait:
                arrived(block, xr.at[p, cc, ch])
            act(remote(block, block, ts.at[cc, ch], xr.at[p, cc, ch], rep=helper))

        others(c, n_c, one)

    def b_rows(slot, g, rr):
        return bbuf.at[slot, g, pl.ds(pl.multiple_of(rr * kb, kb), kb)]

    def bz_copies(act):
        for pp, ee in ((1, 0), (last - 1, last)):
            @pl.when(p != pp)
            def _():
                for slot, part in ((0, pp), (1, ee)):
                    act(remote(
                        bsl.at[part], b_rows(slot, p, r), bzs.at[slot, pp], bzr.at[slot, p], rep=pp))

    def be_copy(g):
        return remote(b_rows(1, g, r), b_rows(0, g, r), bes.at[g], bzr.at[0, g], rep=end)

    def flip(index, bit):
        return index + bit - 2 * bit * lax.rem(lax.div(index, bit), 2)

    steps = []
    held = [()]
    bit = n_r // 2
    while bit:
        steps.append((bit, list(held)))
        held += [flips + (bit,) for flips in held]
        bit //= 2

    def flipped(flips):
        index = r
        for bit in flips:
            index = flip(index, bit)
        return index

    def by_copies(slot, g, step, act):
        bit, blocks = steps[step]
        for flips in blocks:
            rr = flipped(flips)
            block = b_rows(slot, g, rr)
            act(remote(block, block, bys.at[slot, g, step, rr], byr.at[slot, g, rr], row=flip(r, bit)))

    def by_arrived(slot, g, step):
        bit, blocks = steps[step]
        for flips in blocks:
            rr = flipped(flips + (bit,))
            arrived(b_rows(slot, g, rr), byr.at[slot, g, rr])

    def each_slot(f):
        f(0)

        @pl.when(is_mid)
        def _():
            f(1)

    def pass_b(g):
        def one(slot):
            @pl.when(g != p)
            def _():
                arrived(b_rows(slot, g, r), bzr.at[slot, g])

            by_copies(slot, g, 0, start)
            if slot == 1:
                @pl.when(g != end)
                def _():
                    be_copy(g).start()

        each_slot(one)

    def relay_b(g):
        def one(slot):
            for step in range(1, len(steps)):
                by_arrived(slot, g, step - 1)
                by_copies(slot, g, step, start)

        each_slot(one)

    def by_side(d, f):
        @pl.when(p >= d)
        def _():
            f(p - d)

        @pl.when(p + d < n_p)
        def _():
            f(p + d)

    def pass_a(d, low, high):
        @pl.loop(low, high)
        def _(ch):
            def one(g):
                arrived(abuf.at[g, c, ch], zr.at[g, ch])
                z_copies(g, ch, start)
                x_copies(g, ch, start)

            by_side(d, one)

    def send_own(copies, low, high):
        @pl.loop(low, high)
        def _(ch):
            copies(p, ch, start)

    def deg_copy(cc):
        return remote(dego, degr.at[c], ds.at[cc], dr.at[c], col=cc)

    others(c, n_c, lambda cc: deg_copy(cc).start())
    send_own(z_copies, 0, half)
    send_own(x_copies, 0, nch)

    deg = dacc.at[pl.ds(0, kb)]
    deg[...] = 1.0 + dego[...]

    def add_deg(cc):
        arrived(degr.at[cc], dr.at[cc])
        deg[...] += degr[cc]

    others(c, n_c, add_deg)
    for t in range(bm.shape[1] // 128):
        pp, off = divmod(t * 128, cols)
        bsl[pp, :, off:off + 128] = (
            bm[:, t * 128:(t + 1) * 128].astype(jnp.float32) / deg[...]
        ).astype(jnp.bfloat16)
    bz_copies(start)
    mine = pl.ds(pl.multiple_of(r * kb, kb), kb)
    bbuf[0, p, mine] = bsl[p]

    @pl.when(is_mid)
    def _():
        bbuf[1, p, mine] = bsl[end]

    pass_b(p)

    def turn(low, high):
        @pl.when(is_end)
        def _():
            @pl.loop(low, high)
            def _(ch):
                turn_copies(ch, start, True)

    turn(0, half)
    send_own(z_copies, half, nch)
    turn(half, nch)

    def chunk(ch, slots):
        acc[...] = jnp.zeros_like(acc)
        dacc[...] = jnp.ones_like(dacc)
        top = dacc.at[pl.ds(0, ch_rows)]
        for g in range(n_p):
            def one(cc):
                left = abuf[g, cc, ch]
                for slot in range(slots):
                    right = bbuf[slot, g, pl.ds(pl.multiple_of(cc * ka, ka), ka)]
                    acc[slot] += jnp.dot(left, right, preferred_element_type=jnp.float32)
                top[...] += jnp.dot(
                    left, jnp.ones((ka, 128), jnp.bfloat16), preferred_element_type=jnp.float32
                )

            def from_col(cc):
                @pl.when(is_mid | (p != g))
                def _():
                    arrived(abuf.at[g, cc, ch], xr.at[g, cc, ch])

                one(cc)

            one(c)
            others(c, n_c, from_col)
        for i in range(per_ch):
            part = slice(i * width, (i + 1) * width)
            scale = factor / dacc[part]
            at = pl.ds(pl.multiple_of(ch * ch_rows + i * width, width), width)
            for j in range(of.shape[1]):
                tile = slice(j * width, (j + 1) * width)
                flag = of[ch * per_ch + i, j].astype(jnp.float32)
                out[at, tile] = (acc[0, part, tile] * (scale * flag)).astype(jnp.bfloat16)
                if slots == 2:
                    obuf[ch, part, tile] = (acc[1, part, tile] * scale).astype(jnp.bfloat16)

    def o_copy(ch):
        return remote(obuf.at[ch], oin.at[ch], osend.at[ch], orecv.at[ch], rep=end)

    def done_b():
        for g in range(n_p):
            each_slot(lambda slot: by_arrived(slot, g, len(steps) - 1))

    @pl.when(is_end)
    def _():
        relay_b(p)
        for d in range(1, n_p - 1):
            by_side(d, pass_b)
            pass_a(d, half, nch)
            by_side(d, relay_b)
        by_side(n_p - 1, pass_b)
        by_side(n_p - 1, relay_b)
        done_b()

        @pl.loop(half, nch)
        def _(ch):
            pass_a(n_p - 1, ch, ch + 1)

            @pl.when(ch > half)
            def _():
                chunk(ch - 1, 1)

        chunk(nch - 1, 1)

    @pl.when(is_mid)
    def _():
        pass_a(1, 0, half)
        relay_b(p)
        by_side(1, pass_b)
        for d in range(2, n_p - 1):
            pass_a(d, 0, half)
            by_side(d - 1, relay_b)
            by_side(d, pass_b)
        pass_a(1, half, half + 1)
        by_side(n_p - 2, relay_b)
        pass_a(1, half + 1, nch)
        for d in range(2, n_p - 1):
            pass_a(d, half, nch)
        done_b()

        @pl.loop(0, half)
        def _(ch):
            chunk(ch, 2)
            o_copy(ch).start()

        @pl.loop(half, nch)
        def _(ch):
            chunk(ch, 1)

    @pl.when(is_end)
    def _():
        @pl.loop(0, half)
        def _(ch):
            arrived(oin.at[ch], orecv.at[ch])
            for i in range(per_ch):
                at = pl.ds(pl.multiple_of(ch * ch_rows + i * width, width), width)
                for j in range(of.shape[1]):
                    tile = slice(j * width, (j + 1) * width)
                    flag = of[ch * per_ch + i, j].astype(jnp.float32)
                    part = oin[ch, i * width:(i + 1) * width, tile].astype(jnp.float32)
                    out[at, tile] = (part * flag).astype(jnp.bfloat16)

    others(c, n_c, lambda cc: deg_copy(cc).wait_send())
    bz_copies(wait_send)

    @pl.loop(0, n_p)
    def _(g):
        def sent(slot):
            for step in range(len(steps)):
                by_copies(slot, g, step, wait_send)
            if slot == 1:
                @pl.when(g != end)
                def _():
                    be_copy(g).wait_send()

        each_slot(sent)

        @pl.loop(0, nch)
        def _(ch):
            @pl.when((g == p) | is_mid | (ch >= half))
            def _():
                z_copies(g, ch, wait_send)
                x_copies(g, ch, wait_send)

    @pl.when(is_end)
    def _():
        @pl.loop(0, nch)
        def _(ch):
            turn_copies(ch, wait_send, False)

    @pl.when(is_mid)
    def _():
        @pl.loop(0, half)
        def _(ch):
            o_copy(ch).wait_send()


def shards(a_weights, a_flags, b_weights, b_flags, out_flags):
    n_r, n_c, n_p = (lax.axis_size(axis) for axis in ("row", "col", "rep"))
    _, rows, ka = a_weights.shape
    _, kb, wide = b_weights.shape
    cols = wide // n_p
    nch = max(2, 8 // n_c)
    helped = max(1, nch // 4)
    dma = pltpu.SemaphoreType.DMA
    smem = pl.BlockSpec(memory_space=pltpu.SMEM)
    vmem = pl.BlockSpec(memory_space=pltpu.VMEM)
    return pl.pallas_call(
        functools.partial(kernel, n_r, n_c, n_p, nch, float(wide * n_c)),
        out_shape=jax.ShapeDtypeStruct((rows, cols), jnp.bfloat16),
        in_specs=[smem] * 3 + [vmem] * 2,
        out_specs=vmem,
        scratch_shapes=[
            pltpu.VMEM((n_p, n_c, nch, rows // nch, ka), jnp.bfloat16),
            pltpu.VMEM((kb, wide), jnp.bfloat16),
            pltpu.VMEM((n_p, kb, cols), jnp.bfloat16),
            pltpu.VMEM((2, n_p, n_r * kb, cols), jnp.bfloat16),
            pltpu.VMEM((kb, 128), jnp.float32),
            pltpu.VMEM((n_c, kb, 128), jnp.float32),
            pltpu.VMEM((2, rows // nch, cols), jnp.float32),
            pltpu.VMEM((max(kb, rows // nch), 128), jnp.float32),
            pltpu.VMEM((helped, rows // nch, cols), jnp.bfloat16),
            pltpu.VMEM((helped, rows // nch, cols), jnp.bfloat16),
            dma((n_p, nch)), dma((n_p, nch)), dma((n_p, nch)),
            dma((n_p, n_c, nch)), dma((n_p, n_c, nch)), dma((n_c, nch)),
            dma((2, n_p)), dma((2, n_p)), dma((n_p,)),
            dma((2, n_p, n_r)), dma((2, n_p, n_r.bit_length(), n_r)),
            dma((n_c,)), dma((n_c,)),
            dma((helped,)), dma((helped,)),
        ],
        compiler_params=pltpu.CompilerParams(
            collective_id=0, has_side_effects=True, vmem_limit_bytes=56 * 2**20
        ),
    )(a_flags[0], b_flags[0], out_flags, a_weights[0], b_weights[0])


def solution(mesh):
    return jax.shard_map(
        shards,
        mesh=mesh,
        in_specs=(
            P("rep", "row", "col"),
            P("rep", "row", "col"),
            P("rep", "row", "col"),
            P("rep", "row", "col"),
            P("row", ("col", "rep")),
        ),
        out_specs=P("row", ("col", "rep")),
        check_vma=False,
    )
```

```python
import functools

import jax
import jax.numpy as jnp
from jax import lax
from jax.experimental import pallas as pl
from jax.experimental.pallas import tpu as pltpu
from jax.sharding import PartitionSpec as P

MESH = pl.DeviceIdType.MESH


def kernel(
    n_r, n_c, n_p, nch,
    af_in, bf_in, of_in, a_in, b_in, out,
    af, bf, of, a, b, loads, abuf, bm, bsl, bbuf, dego, degr, acc, dacc,
    zr, zsl, zsr, xr, xs, ts, bzr, bzs, byr, bys, dr, ds,
):
    r, c, p = lax.axis_index("row"), lax.axis_index("col"), lax.axis_index("rep")
    rows, ka = a.shape
    kb = b.shape[0]
    width = rows // af.shape[1]
    cols = out.shape[1]
    ch_rows = rows // nch
    last = n_p - 1
    turns = n_p >= 4
    is_end = (p == 0) | (p == last)
    inner = 1 + lax.div(p, n_p // 2) * (last - 2)

    copies = [
        pltpu.make_async_copy(src, dst, loads.at[k])
        for k, (src, dst) in enumerate(
            ((bf_in, bf), (b_in, b), (af_in, af), (a_in, a), (of_in, of)))
    ]
    for copy in copies:
        copy.start()

    barrier = pltpu.get_barrier_semaphore()
    for axis, mine, count in (("row", r, n_r), ("col", c, n_c), ("rep", p, n_p)):
        for o in range(1, count):
            pl.semaphore_signal(
                barrier, inc=1, device_id={axis: lax.rem(mine + o, count)}, device_id_type=MESH
            )

    for copy in copies:
        copy.wait()

    for i in range(bf.shape[0]):
        for j in range(bf.shape[1]):
            at = (slice(i * width, (i + 1) * width), slice(j * width, (j + 1) * width))
            bm[at] = (b[at].astype(jnp.float32) * bf[i, j].astype(jnp.float32)).astype(jnp.bfloat16)
    dego[...] = jnp.dot(
        bm[...], jnp.ones((bm.shape[1], 128), jnp.bfloat16), preferred_element_type=jnp.float32
    )
    for i in range(af.shape[1]):
        ch, off = divmod(i * width, ch_rows)
        for j in range(af.shape[0]):
            tile = a[i * width:(i + 1) * width, j * width:(j + 1) * width].astype(jnp.float32)
            abuf[p, c, ch, off:off + width, j * width:(j + 1) * width] = (
                tile * af[j, i].astype(jnp.float32)
            ).astype(jnp.bfloat16)

    pl.semaphore_wait(barrier, n_r + n_c + n_p - 3)

    def deg_copy(cc):
        return pltpu.make_async_remote_copy(
            src_ref=dego, dst_ref=degr.at[c], send_sem=ds.at[cc], recv_sem=dr.at[c],
            device_id={"col": cc}, device_id_type=MESH)

    def z_copy(g, ch, to, send):
        block = abuf.at[g, c, ch]
        return pltpu.make_async_remote_copy(
            src_ref=block, dst_ref=block, send_sem=send.at[g, ch], recv_sem=zr.at[g, ch],
            device_id={"rep": to}, device_id_type=MESH)

    def x_copy(g, ch, cc):
        block = abuf.at[g, c, ch]
        return pltpu.make_async_remote_copy(
            src_ref=block, dst_ref=block, send_sem=xs.at[g, cc, ch], recv_sem=xr.at[g, c, ch],
            device_id={"col": cc}, device_id_type=MESH)

    def bz_copy(pp):
        return pltpu.make_async_remote_copy(
            src_ref=bsl.at[pp], dst_ref=bbuf.at[p, pl.ds(pl.multiple_of(r * kb, kb), kb)],
            send_sem=bzs.at[pp], recv_sem=bzr.at[p], device_id={"rep": pp}, device_id_type=MESH)

    def by_copy(g, rr):
        block = bbuf.at[g, pl.ds(pl.multiple_of(r * kb, kb), kb)]
        return pltpu.make_async_remote_copy(
            src_ref=block, dst_ref=block, send_sem=bys.at[g, rr], recv_sem=byr.at[g, r],
            device_id={"row": rr}, device_id_type=MESH)

    def arrived(ref, sem):
        pltpu.make_async_copy(ref, ref, sem).wait()

    def others(mine, count, f):
        @pl.loop(1, count)
        def _(o):
            f(lax.rem(mine + o, count))

    def crosses(g):
        if not turns:
            return g >= 0
        return ((p != 1) | (g != 0)) & ((p != last - 1) | (g != last))

    def forward(g, ch):
        @pl.when(crosses(g))
        def _():
            others(c, n_c, lambda cc: x_copy(g, ch, cc).start())

    def turn_copy(cc, ch):
        block = abuf.at[p, cc, ch]
        return pltpu.make_async_remote_copy(
            src_ref=block, dst_ref=block, send_sem=ts.at[cc, ch], recv_sem=xr.at[p, cc, ch],
            device_id={"rep": inner}, device_id_type=MESH)

    def turn(ch):
        def one(cc):
            arrived(abuf.at[p, cc, ch], xr.at[p, cc, ch])
            turn_copy(cc, ch).start()

        @pl.when(is_end)
        def _():
            others(c, n_c, one)

    others(c, n_c, lambda cc: deg_copy(cc).start())

    @pl.loop(0, nch)
    def _(ch):
        @pl.when(p > 0)
        def _():
            z_copy(p, ch, p - 1, zsl).start()

        @pl.when(p < n_p - 1)
        def _():
            z_copy(p, ch, p + 1, zsr).start()

        forward(p, ch)

    def add_deg(cc):
        arrived(degr.at[cc], dr.at[cc])
        dego_sum[...] += degr[cc]

    dego_sum = dacc.at[pl.ds(0, kb)]
    dego_sum[...] = 1.0 + dego[...]
    others(c, n_c, add_deg)
    for t in range(bm.shape[1] // 128):
        pp, off = divmod(t * 128, cols)
        bsl[pp, :, off:off + 128] = (
            bm[:, t * 128:(t + 1) * 128].astype(jnp.float32) / dego_sum[...]
        ).astype(jnp.bfloat16)
    others(p, n_p, lambda pp: bz_copy(pp).start())
    bbuf[p, pl.ds(pl.multiple_of(r * kb, kb), kb)] = bsl[p]
    others(r, n_r, lambda rr: by_copy(p, rr).start())

    acc[...] = jnp.zeros_like(acc)
    dacc[...] = jnp.ones_like(dacc)

    def by_side(d, f):
        @pl.when(p >= d)
        def _():
            f(p - d)

        if d:
            @pl.when(p + d < n_p)
            def _():
                f(p + d)

    def block(g, cc, ch):
        left = abuf[g, cc, ch]
        right = bbuf[g, pl.ds(pl.multiple_of(cc * ka, ka), ka)]
        at = pl.ds(pl.multiple_of(ch * ch_rows, ch_rows), ch_rows)
        acc[at] += jnp.dot(left, right, preferred_element_type=jnp.float32)
        dacc[at] += jnp.dot(
            left, jnp.ones((ka, 128), jnp.bfloat16), preferred_element_type=jnp.float32
        )

    def own(d, ch):
        def one(g):
            @pl.when(ch == 0)
            def _():
                others(r, n_r, lambda rr: arrived(
                    bbuf.at[g, pl.ds(pl.multiple_of(rr * kb, kb), kb)], byr.at[g, rr]))

            block(g, c, ch)

        by_side(d, one)

    def crossed(d, ch):
        def one(g):
            def from_col(cc):
                @pl.when((g != p) | ~is_end if turns else g >= 0)
                def _():
                    arrived(abuf.at[g, cc, ch], xr.at[g, cc, ch])

                block(g, cc, ch)

            others(c, n_c, from_col)

        by_side(d, one)

    for d in range(1, n_p + 2):
        @pl.loop(0, nch)
        def _(ch):
            def pass_a(g):
                arrived(abuf.at[g, c, ch], zr.at[g, ch])

                @pl.when((g < p) & (p < n_p - 1))
                def _():
                    z_copy(g, ch, p + 1, zsr).start()

                @pl.when((g > p) & (p > 0))
                def _():
                    z_copy(g, ch, p - 1, zsl).start()

                forward(g, ch)

            if d < n_p:
                by_side(d, pass_a)
            if d == 1 and turns:
                turn(ch)
            if d <= n_p:
                own(d - 1, ch)
            if d >= 2:
                crossed(d - 2, ch)

        def pass_b(g):
            arrived(bbuf.at[g, pl.ds(pl.multiple_of(r * kb, kb), kb)], bzr.at[g])
            others(r, n_r, lambda rr: by_copy(g, rr).start())

        if d < n_p:
            by_side(d, pass_b)

    @pl.loop(0, of.shape[1])
    def _(i):
        at = pl.ds(pl.multiple_of(i * width, width), width)
        scale = 1.0 / dacc[at]
        for j in range(of.shape[0]):
            tile = slice(j * width, (j + 1) * width)
            out[at, tile] = (
                acc[at, tile] * (scale * of[j, i].astype(jnp.float32))
            ).astype(jnp.bfloat16)

    if turns:
        @pl.when(is_end)
        def _():
            @pl.loop(0, nch)
            def _(ch):
                others(c, n_c, lambda cc: turn_copy(cc, ch).wait_send())

    others(c, n_c, lambda cc: deg_copy(cc).wait_send())
    others(p, n_p, lambda pp: bz_copy(pp).wait_send())

    @pl.loop(0, n_p)
    def _(g):
        others(r, n_r, lambda rr: by_copy(g, rr).wait_send())

        @pl.loop(0, nch)
        def _(ch):
            @pl.when(crosses(g))
            def _():
                others(c, n_c, lambda cc: x_copy(g, ch, cc).wait_send())

            @pl.when((g >= p) & (p > 0))
            def _():
                z_copy(g, ch, p - 1, zsl).wait_send()

            @pl.when((g <= p) & (p < n_p - 1))
            def _():
                z_copy(g, ch, p + 1, zsr).wait_send()


def shards(a_weights, a_flags, b_weights, b_flags, out_flags):
    n_r, n_c, n_p = (lax.axis_size(axis) for axis in ("row", "col", "rep"))
    _, rows, ka = a_weights.shape
    _, kb, wide = b_weights.shape
    cols = wide // n_p
    nch = max(1, 8 // n_c)
    dma = pltpu.SemaphoreType.DMA
    operands = (a_flags[0].T, b_flags[0], out_flags.T, a_weights[0], b_weights[0])
    density = pl.pallas_call(
        functools.partial(kernel, n_r, n_c, n_p, nch),
        out_shape=jax.ShapeDtypeStruct((rows, cols), jnp.bfloat16),
        in_specs=[pl.BlockSpec(memory_space=pl.ANY)] * 5,
        out_specs=pl.BlockSpec(memory_space=pltpu.VMEM),
        scratch_shapes=[
            *(pltpu.SMEM(x.shape, x.dtype) for x in operands[:3]),
            *(pltpu.VMEM(x.shape, x.dtype) for x in operands[3:]),
            dma((5,)),
            pltpu.VMEM((n_p, n_c, nch, rows // nch, ka), jnp.bfloat16),
            pltpu.VMEM((kb, wide), jnp.bfloat16),
            pltpu.VMEM((n_p, kb, cols), jnp.bfloat16),
            pltpu.VMEM((n_p, n_r * kb, cols), jnp.bfloat16),
            pltpu.VMEM((kb, 128), jnp.float32),
            pltpu.VMEM((n_c, kb, 128), jnp.float32),
            pltpu.VMEM((rows, cols), jnp.float32),
            pltpu.VMEM((rows, 128), jnp.float32),
            dma((n_p, nch)), dma((n_p, nch)), dma((n_p, nch)),
            dma((n_p, n_c, nch)), dma((n_p, n_c, nch)), dma((n_c, nch)),
            dma((n_p,)), dma((n_p,)),
            dma((n_p, n_r)), dma((n_p, n_r)),
            dma((n_c,)), dma((n_c,)),
        ],
        compiler_params=pltpu.CompilerParams(
            collective_id=0, has_side_effects=True, vmem_limit_bytes=56 * 2**20
        ),
    )(*operands)
    factor = jnp.float32(wide * n_c)
    return (factor * density.astype(jnp.float32)).astype(jnp.bfloat16)


def solution(mesh):
    return jax.shard_map(
        shards,
        mesh=mesh,
        in_specs=(
            P("rep", "row", "col"),
            P("rep", "row", "col"),
            P("rep", "row", "col"),
            P("rep", "row", "col"),
            P("row", ("col", "rep")),
        ),
        out_specs=P("row", ("col", "rep")),
        check_vma=False,
    )
```

```python
import functools

import jax
import jax.numpy as jnp
from jax import lax
from jax.experimental import pallas as pl
from jax.experimental.pallas import tpu as pltpu
from jax.sharding import PartitionSpec as P

MESH = pl.DeviceIdType.MESH


def kernel(
    n_r, n_c, n_p, nch,
    af_in, bf_in, of_in, a_in, b_in, out,
    af, bf, of, a, b, loads, abuf, bm, bsl, bbuf, dego, degr, acc, dacc,
    zr, zsl, zsr, xr, xs, ts, bzr, bzs, byr, bys, dr, ds,
):
    r, c, p = lax.axis_index("row"), lax.axis_index("col"), lax.axis_index("rep")
    rows, ka = a.shape
    kb = b.shape[0]
    width = rows // af.shape[1]
    cols = out.shape[1]
    ch_rows = rows // nch
    last = n_p - 1
    turns = n_p >= 4
    is_end = (p == 0) | (p == last)
    inner = 1 + lax.div(p, n_p // 2) * (last - 2)

    barrier = pltpu.get_barrier_semaphore()
    for axis, mine, count in (("row", r, n_r), ("col", c, n_c), ("rep", p, n_p)):
        for o in range(1, count):
            pl.semaphore_signal(
                barrier, inc=1, device_id={axis: lax.rem(mine + o, count)}, device_id_type=MESH
            )

    copies = [
        pltpu.make_async_copy(src, dst, loads.at[k])
        for k, (src, dst) in enumerate(
            ((af_in, af), (a_in, a), (bf_in, bf), (b_in, b), (of_in, of)))
    ]
    for copy in copies:
        copy.start()

    for copy in copies[:2]:
        copy.wait()

    for i in range(af.shape[1]):
        ch, off = divmod(i * width, ch_rows)
        for j in range(af.shape[0]):
            tile = a[i * width:(i + 1) * width, j * width:(j + 1) * width].astype(jnp.float32)
            abuf[p, c, ch, off:off + width, j * width:(j + 1) * width] = (
                tile * af[j, i].astype(jnp.float32)
            ).astype(jnp.bfloat16)

    pl.semaphore_wait(barrier, n_r + n_c + n_p - 3)

    def deg_copy(cc):
        return pltpu.make_async_remote_copy(
            src_ref=dego, dst_ref=degr.at[c], send_sem=ds.at[cc], recv_sem=dr.at[c],
            device_id={"col": cc}, device_id_type=MESH)

    def z_copy(g, ch, to, send):
        block = abuf.at[g, c, ch]
        return pltpu.make_async_remote_copy(
            src_ref=block, dst_ref=block, send_sem=send.at[g, ch], recv_sem=zr.at[g, ch],
            device_id={"rep": to}, device_id_type=MESH)

    def x_copy(g, ch, cc):
        block = abuf.at[g, c, ch]
        return pltpu.make_async_remote_copy(
            src_ref=block, dst_ref=block, send_sem=xs.at[g, cc, ch], recv_sem=xr.at[g, c, ch],
            device_id={"col": cc}, device_id_type=MESH)

    def bz_copy(pp):
        return pltpu.make_async_remote_copy(
            src_ref=bsl.at[pp], dst_ref=bbuf.at[p, pl.ds(pl.multiple_of(r * kb, kb), kb)],
            send_sem=bzs.at[pp], recv_sem=bzr.at[p], device_id={"rep": pp}, device_id_type=MESH)

    def by_copy(g, rr):
        block = bbuf.at[g, pl.ds(pl.multiple_of(r * kb, kb), kb)]
        return pltpu.make_async_remote_copy(
            src_ref=block, dst_ref=block, send_sem=bys.at[g, rr], recv_sem=byr.at[g, r],
            device_id={"row": rr}, device_id_type=MESH)

    def arrived(ref, sem):
        pltpu.make_async_copy(ref, ref, sem).wait()

    def others(mine, count, f):
        @pl.loop(1, count)
        def _(o):
            f(lax.rem(mine + o, count))

    def crosses(g):
        if not turns:
            return g >= 0
        return ((p != 1) | (g != 0)) & ((p != last - 1) | (g != last))

    def forward(g, ch):
        @pl.when(crosses(g))
        def _():
            others(c, n_c, lambda cc: x_copy(g, ch, cc).start())

    def turn_copy(cc, ch):
        block = abuf.at[p, cc, ch]
        return pltpu.make_async_remote_copy(
            src_ref=block, dst_ref=block, send_sem=ts.at[cc, ch], recv_sem=xr.at[p, cc, ch],
            device_id={"rep": inner}, device_id_type=MESH)

    def turn(ch):
        def one(cc):
            arrived(abuf.at[p, cc, ch], xr.at[p, cc, ch])
            turn_copy(cc, ch).start()

        @pl.when(is_end)
        def _():
            others(c, n_c, one)

    @pl.loop(0, nch)
    def _(ch):
        @pl.when(p > 0)
        def _():
            z_copy(p, ch, p - 1, zsl).start()

        @pl.when(p < n_p - 1)
        def _():
            z_copy(p, ch, p + 1, zsr).start()

    for copy in copies[2:]:
        copy.wait()

    for i in range(bf.shape[0]):
        for j in range(bf.shape[1]):
            at = (slice(i * width, (i + 1) * width), slice(j * width, (j + 1) * width))
            bm[at] = (b[at].astype(jnp.float32) * bf[i, j].astype(jnp.float32)).astype(jnp.bfloat16)
    dego[...] = jnp.dot(
        bm[...], jnp.ones((bm.shape[1], 128), jnp.bfloat16), preferred_element_type=jnp.float32
    )
    others(c, n_c, lambda cc: deg_copy(cc).start())

    @pl.loop(0, nch)
    def _(ch):
        forward(p, ch)

    def add_deg(cc):
        arrived(degr.at[cc], dr.at[cc])
        dego_sum[...] += degr[cc]

    dego_sum = dacc.at[pl.ds(0, kb)]
    dego_sum[...] = 1.0 + dego[...]
    others(c, n_c, add_deg)
    for t in range(bm.shape[1] // 128):
        pp, off = divmod(t * 128, cols)
        bsl[pp, :, off:off + 128] = (
            bm[:, t * 128:(t + 1) * 128].astype(jnp.float32) / dego_sum[...]
        ).astype(jnp.bfloat16)
    others(p, n_p, lambda pp: bz_copy(pp).start())
    bbuf[p, pl.ds(pl.multiple_of(r * kb, kb), kb)] = bsl[p]
    others(r, n_r, lambda rr: by_copy(p, rr).start())

    acc[...] = jnp.zeros_like(acc)
    dacc[...] = jnp.ones_like(dacc)

    def by_side(d, f):
        @pl.when(p >= d)
        def _():
            f(p - d)

        if d:
            @pl.when(p + d < n_p)
            def _():
                f(p + d)

    def block(g, cc, ch):
        left = abuf[g, cc, ch]
        right = bbuf[g, pl.ds(pl.multiple_of(cc * ka, ka), ka)]
        at = pl.ds(pl.multiple_of(ch * ch_rows, ch_rows), ch_rows)
        acc[at] += jnp.dot(left, right, preferred_element_type=jnp.float32)
        dacc[at] += jnp.dot(
            left, jnp.ones((ka, 128), jnp.bfloat16), preferred_element_type=jnp.float32
        )

    def own(d, ch):
        def one(g):
            @pl.when(ch == 0)
            def _():
                others(r, n_r, lambda rr: arrived(
                    bbuf.at[g, pl.ds(pl.multiple_of(rr * kb, kb), kb)], byr.at[g, rr]))

            block(g, c, ch)

        by_side(d, one)

    def crossed(d, ch):
        def one(g):
            def from_col(cc):
                @pl.when((g != p) | ~is_end if turns else g >= 0)
                def _():
                    arrived(abuf.at[g, cc, ch], xr.at[g, cc, ch])

                block(g, cc, ch)

            others(c, n_c, from_col)

        by_side(d, one)

    def pass_b(g):
        arrived(bbuf.at[g, pl.ds(pl.multiple_of(r * kb, kb), kb)], bzr.at[g])
        others(r, n_r, lambda rr: by_copy(g, rr).start())

    def finish(i):
        at = pl.ds(pl.multiple_of(i * width, width), width)
        scale = 1.0 / dacc[at]
        for j in range(of.shape[0]):
            tile = slice(j * width, (j + 1) * width)
            out[at, tile] = (
                acc[at, tile] * (scale * of[j, i].astype(jnp.float32))
            ).astype(jnp.bfloat16)

    for d in range(1, n_p + 1):
        if 1 < d < n_p:
            by_side(d, pass_b)

        @pl.loop(0, nch)
        def _(ch):
            def pass_a(g):
                arrived(abuf.at[g, c, ch], zr.at[g, ch])

                @pl.when((g < p) & (p < n_p - 1))
                def _():
                    z_copy(g, ch, p + 1, zsr).start()

                @pl.when((g > p) & (p > 0))
                def _():
                    z_copy(g, ch, p - 1, zsl).start()

                forward(g, ch)

            if d < n_p:
                by_side(d, pass_a)
            if d == 1:
                if turns:
                    turn(ch)
                own(0, ch)
            if d == 2:
                own(1, ch)
                crossed(0, ch)
            if 1 < d <= n_p:
                crossed(d - 1, ch)
            if 1 < d < n_p:
                own(d, ch)
            if d == n_p:
                for i in range(ch_rows // width):
                    finish(ch * (ch_rows // width) + i)

        if d == 1:
            by_side(1, pass_b)

    if turns:
        @pl.when(is_end)
        def _():
            @pl.loop(0, nch)
            def _(ch):
                others(c, n_c, lambda cc: turn_copy(cc, ch).wait_send())

    others(c, n_c, lambda cc: deg_copy(cc).wait_send())
    others(p, n_p, lambda pp: bz_copy(pp).wait_send())

    @pl.loop(0, n_p)
    def _(g):
        others(r, n_r, lambda rr: by_copy(g, rr).wait_send())

        @pl.loop(0, nch)
        def _(ch):
            @pl.when(crosses(g))
            def _():
                others(c, n_c, lambda cc: x_copy(g, ch, cc).wait_send())

            @pl.when((g >= p) & (p > 0))
            def _():
                z_copy(g, ch, p - 1, zsl).wait_send()

            @pl.when((g <= p) & (p < n_p - 1))
            def _():
                z_copy(g, ch, p + 1, zsr).wait_send()


def shards(a_weights, a_flags, b_weights, b_flags, out_flags):
    n_r, n_c, n_p = (lax.axis_size(axis) for axis in ("row", "col", "rep"))
    _, rows, ka = a_weights.shape
    _, kb, wide = b_weights.shape
    cols = wide // n_p
    nch = max(1, 8 // n_c)
    dma = pltpu.SemaphoreType.DMA
    operands = (a_flags[0].T, b_flags[0], out_flags.T, a_weights[0], b_weights[0])
    density = pl.pallas_call(
        functools.partial(kernel, n_r, n_c, n_p, nch),
        out_shape=jax.ShapeDtypeStruct((rows, cols), jnp.bfloat16),
        in_specs=[pl.BlockSpec(memory_space=pl.ANY)] * 5,
        out_specs=pl.BlockSpec(memory_space=pltpu.VMEM),
        scratch_shapes=[
            *(pltpu.SMEM(x.shape, x.dtype) for x in operands[:3]),
            *(pltpu.VMEM(x.shape, x.dtype) for x in operands[3:]),
            dma((5,)),
            pltpu.VMEM((n_p, n_c, nch, rows // nch, ka), jnp.bfloat16),
            pltpu.VMEM((kb, wide), jnp.bfloat16),
            pltpu.VMEM((n_p, kb, cols), jnp.bfloat16),
            pltpu.VMEM((n_p, n_r * kb, cols), jnp.bfloat16),
            pltpu.VMEM((kb, 128), jnp.float32),
            pltpu.VMEM((n_c, kb, 128), jnp.float32),
            pltpu.VMEM((rows, cols), jnp.float32),
            pltpu.VMEM((rows, 128), jnp.float32),
            dma((n_p, nch)), dma((n_p, nch)), dma((n_p, nch)),
            dma((n_p, n_c, nch)), dma((n_p, n_c, nch)), dma((n_c, nch)),
            dma((n_p,)), dma((n_p,)),
            dma((n_p, n_r)), dma((n_p, n_r)),
            dma((n_c,)), dma((n_c,)),
        ],
        compiler_params=pltpu.CompilerParams(
            collective_id=0, has_side_effects=True, vmem_limit_bytes=56 * 2**20
        ),
    )(*operands)
    factor = jnp.float32(wide * n_c)
    return (factor * density.astype(jnp.float32)).astype(jnp.bfloat16)


def solution(mesh):
    return jax.shard_map(
        shards,
        mesh=mesh,
        in_specs=(
            P("rep", "row", "col"),
            P("rep", "row", "col"),
            P("rep", "row", "col"),
            P("rep", "row", "col"),
            P("row", ("col", "rep")),
        ),
        out_specs=P("row", ("col", "rep")),
        check_vma=False,
    )
```

```python
import functools

import jax
import jax.numpy as jnp
from jax import lax
from jax.experimental import pallas as pl
from jax.experimental.pallas import tpu as pltpu
from jax.sharding import PartitionSpec as P

MESH = pl.DeviceIdType.MESH


def kernel(
    n_r, n_c, n_p, nch,
    af_in, bf_in, of_in, a_in, b_in, out,
    af, bf, of, a, b, loads, abuf, bm, bsl, bbuf, dego, degr, acc, dacc,
    zr, zsl, zsr, xr, xs, ts, bzr, bzs, byr, bys, dr, ds,
):
    r, c, p = lax.axis_index("row"), lax.axis_index("col"), lax.axis_index("rep")
    rows, ka = a.shape
    kb = b.shape[0]
    width = rows // af.shape[1]
    cols = out.shape[1]
    ch_rows = rows // nch
    last = n_p - 1
    turns = n_p >= 4
    is_end = (p == 0) | (p == last)
    inner = 1 + lax.div(p, n_p // 2) * (last - 2)

    barrier = pltpu.get_barrier_semaphore()
    for axis, mine, count in (("row", r, n_r), ("col", c, n_c), ("rep", p, n_p)):
        for o in range(1, count):
            pl.semaphore_signal(
                barrier, inc=1, device_id={axis: lax.rem(mine + o, count)}, device_id_type=MESH
            )

    copies = [
        pltpu.make_async_copy(src, dst, loads.at[k])
        for k, (src, dst) in enumerate(
            ((af_in, af), (a_in, a), (bf_in, bf), (b_in, b), (of_in, of)))
    ]
    for copy in copies:
        copy.start()

    for copy in copies[:2]:
        copy.wait()

    for i in range(af.shape[1]):
        ch, off = divmod(i * width, ch_rows)
        for j in range(af.shape[0]):
            tile = a[i * width:(i + 1) * width, j * width:(j + 1) * width].astype(jnp.float32)
            abuf[p, c, ch, off:off + width, j * width:(j + 1) * width] = (
                tile * af[j, i].astype(jnp.float32)
            ).astype(jnp.bfloat16)

    pl.semaphore_wait(barrier, n_r + n_c + n_p - 3)

    def deg_copy(cc):
        return pltpu.make_async_remote_copy(
            src_ref=dego, dst_ref=degr.at[c], send_sem=ds.at[cc], recv_sem=dr.at[c],
            device_id={"col": cc}, device_id_type=MESH)

    def z_copy(g, ch, to, send):
        block = abuf.at[g, c, ch]
        return pltpu.make_async_remote_copy(
            src_ref=block, dst_ref=block, send_sem=send.at[g, ch], recv_sem=zr.at[g, ch],
            device_id={"rep": to}, device_id_type=MESH)

    def x_copy(g, ch, cc):
        block = abuf.at[g, c, ch]
        return pltpu.make_async_remote_copy(
            src_ref=block, dst_ref=block, send_sem=xs.at[g, cc, ch], recv_sem=xr.at[g, c, ch],
            device_id={"col": cc}, device_id_type=MESH)

    def bz_copy(pp):
        return pltpu.make_async_remote_copy(
            src_ref=bsl.at[pp], dst_ref=bbuf.at[p, pl.ds(pl.multiple_of(r * kb, kb), kb)],
            send_sem=bzs.at[pp], recv_sem=bzr.at[p], device_id={"rep": pp}, device_id_type=MESH)

    def by_copy(g, rr):
        block = bbuf.at[g, pl.ds(pl.multiple_of(r * kb, kb), kb)]
        return pltpu.make_async_remote_copy(
            src_ref=block, dst_ref=block, send_sem=bys.at[g, rr], recv_sem=byr.at[g, r],
            device_id={"row": rr}, device_id_type=MESH)

    def arrived(ref, sem):
        pltpu.make_async_copy(ref, ref, sem).wait()

    def others(mine, count, f):
        @pl.loop(1, count)
        def _(o):
            f(lax.rem(mine + o, count))

    def crosses(g):
        if not turns:
            return g >= 0
        return ((p != 1) | (g != 0)) & ((p != last - 1) | (g != last))

    def forward(g, ch):
        @pl.when(crosses(g))
        def _():
            others(c, n_c, lambda cc: x_copy(g, ch, cc).start())

    def turn_copy(cc, ch):
        block = abuf.at[p, cc, ch]
        return pltpu.make_async_remote_copy(
            src_ref=block, dst_ref=block, send_sem=ts.at[cc, ch], recv_sem=xr.at[p, cc, ch],
            device_id={"rep": inner}, device_id_type=MESH)

    def turn(ch):
        def one(cc):
            arrived(abuf.at[p, cc, ch], xr.at[p, cc, ch])
            turn_copy(cc, ch).start()

        @pl.when(is_end)
        def _():
            others(c, n_c, one)

    @pl.loop(0, nch)
    def _(ch):
        @pl.when(p > 0)
        def _():
            z_copy(p, ch, p - 1, zsl).start()

        @pl.when(p < n_p - 1)
        def _():
            z_copy(p, ch, p + 1, zsr).start()

    for copy in copies[2:]:
        copy.wait()

    for i in range(bf.shape[0]):
        for j in range(bf.shape[1]):
            at = (slice(i * width, (i + 1) * width), slice(j * width, (j + 1) * width))
            bm[at] = (b[at].astype(jnp.float32) * bf[i, j].astype(jnp.float32)).astype(jnp.bfloat16)
    dego[...] = jnp.dot(
        bm[...], jnp.ones((bm.shape[1], 128), jnp.bfloat16), preferred_element_type=jnp.float32
    )
    others(c, n_c, lambda cc: deg_copy(cc).start())

    @pl.loop(0, nch)
    def _(ch):
        forward(p, ch)

    def add_deg(cc):
        arrived(degr.at[cc], dr.at[cc])
        dego_sum[...] += degr[cc]

    dego_sum = dacc.at[pl.ds(0, kb)]
    dego_sum[...] = 1.0 + dego[...]
    others(c, n_c, add_deg)
    for t in range(bm.shape[1] // 128):
        pp, off = divmod(t * 128, cols)
        bsl[pp, :, off:off + 128] = (
            bm[:, t * 128:(t + 1) * 128].astype(jnp.float32) / dego_sum[...]
        ).astype(jnp.bfloat16)
    others(p, n_p, lambda pp: bz_copy(pp).start())
    bbuf[p, pl.ds(pl.multiple_of(r * kb, kb), kb)] = bsl[p]
    others(r, n_r, lambda rr: by_copy(p, rr).start())

    acc[...] = jnp.zeros_like(acc)
    dacc[...] = jnp.ones_like(dacc)

    def by_side(d, f):
        @pl.when(p >= d)
        def _():
            f(p - d)

        if d:
            @pl.when(p + d < n_p)
            def _():
                f(p + d)

    def block(g, cc, ch):
        left = abuf[g, cc, ch]
        right = bbuf[g, pl.ds(pl.multiple_of(cc * ka, ka), ka)]
        at = pl.ds(pl.multiple_of(ch * ch_rows, ch_rows), ch_rows)
        acc[at] += jnp.dot(left, right, preferred_element_type=jnp.float32)
        dacc[at] += jnp.dot(
            left, jnp.ones((ka, 128), jnp.bfloat16), preferred_element_type=jnp.float32
        )

    def own(d, ch):
        def one(g):
            @pl.when(ch == 0)
            def _():
                others(r, n_r, lambda rr: arrived(
                    bbuf.at[g, pl.ds(pl.multiple_of(rr * kb, kb), kb)], byr.at[g, rr]))

            block(g, c, ch)

        by_side(d, one)

    def crossed(d, ch):
        def one(g):
            def from_col(cc):
                @pl.when((g != p) | ~is_end if turns else g >= 0)
                def _():
                    arrived(abuf.at[g, cc, ch], xr.at[g, cc, ch])

                block(g, cc, ch)

            others(c, n_c, from_col)

        by_side(d, one)

    def pass_b(g):
        arrived(bbuf.at[g, pl.ds(pl.multiple_of(r * kb, kb), kb)], bzr.at[g])
        others(r, n_r, lambda rr: by_copy(g, rr).start())

    def finish(i):
        at = pl.ds(pl.multiple_of(i * width, width), width)
        scale = 1.0 / dacc[at]
        for j in range(of.shape[0]):
            tile = slice(j * width, (j + 1) * width)
            out[at, tile] = (
                acc[at, tile] * (scale * of[j, i].astype(jnp.float32))
            ).astype(jnp.bfloat16)

    for d in range(1, n_p + 1):
        if 1 < d < n_p:
            by_side(d, pass_b)

        @pl.loop(0, nch)
        def _(ch):
            def pass_a(g):
                arrived(abuf.at[g, c, ch], zr.at[g, ch])

                @pl.when((g < p) & (p < n_p - 1))
                def _():
                    z_copy(g, ch, p + 1, zsr).start()

                @pl.when((g > p) & (p > 0))
                def _():
                    z_copy(g, ch, p - 1, zsl).start()

                forward(g, ch)

            if d < n_p:
                by_side(d, pass_a)
            if d == 1:
                if turns:
                    turn(ch)
                own(0, ch)
            if d == 2:
                own(1, ch)
                crossed(0, ch)
            if 1 < d <= n_p:
                crossed(d - 1, ch)
            if 1 < d < n_p:
                own(d, ch)
            if d == n_p:
                for i in range(ch_rows // width):
                    finish(ch * (ch_rows // width) + i)

        if d == 1:
            by_side(1, pass_b)

    if turns:
        @pl.when(is_end)
        def _():
            @pl.loop(0, nch)
            def _(ch):
                others(c, n_c, lambda cc: turn_copy(cc, ch).wait_send())

    others(c, n_c, lambda cc: deg_copy(cc).wait_send())
    others(p, n_p, lambda pp: bz_copy(pp).wait_send())

    @pl.loop(0, n_p)
    def _(g):
        others(r, n_r, lambda rr: by_copy(g, rr).wait_send())

        @pl.loop(0, nch)
        def _(ch):
            @pl.when(crosses(g))
            def _():
                others(c, n_c, lambda cc: x_copy(g, ch, cc).wait_send())

            @pl.when((g >= p) & (p > 0))
            def _():
                z_copy(g, ch, p - 1, zsl).wait_send()

            @pl.when((g <= p) & (p < n_p - 1))
            def _():
                z_copy(g, ch, p + 1, zsr).wait_send()


def shards(a_weights, a_flags, b_weights, b_flags, out_flags):
    n_r, n_c, n_p = (lax.axis_size(axis) for axis in ("row", "col", "rep"))
    _, rows, ka = a_weights.shape
    _, kb, wide = b_weights.shape
    cols = wide // n_p
    nch = max(1, 8 // n_c)
    dma = pltpu.SemaphoreType.DMA
    operands = (a_flags[0].T, b_flags[0], out_flags.T, a_weights[0], b_weights[0])
    held = 2 * (rows * ka * (n_p * n_c + 1) + kb * wide * 3 + n_p * n_r * kb * cols + rows * cols)
    held += 4 * (kb * 128 * (n_c + 1) + rows * (cols + 128))
    density = pl.pallas_call(
        functools.partial(kernel, n_r, n_c, n_p, nch),
        out_shape=jax.ShapeDtypeStruct((rows, cols), jnp.bfloat16),
        in_specs=[pl.BlockSpec(memory_space=pltpu.HBM)] * 5,
        out_specs=pl.BlockSpec(memory_space=pltpu.VMEM),
        scratch_shapes=[
            *(pltpu.SMEM(x.shape, x.dtype) for x in operands[:3]),
            *(pltpu.VMEM(x.shape, x.dtype) for x in operands[3:]),
            dma((5,)),
            pltpu.VMEM((n_p, n_c, nch, rows // nch, ka), jnp.bfloat16),
            pltpu.VMEM((kb, wide), jnp.bfloat16),
            pltpu.VMEM((n_p, kb, cols), jnp.bfloat16),
            pltpu.VMEM((n_p, n_r * kb, cols), jnp.bfloat16),
            pltpu.VMEM((kb, 128), jnp.float32),
            pltpu.VMEM((n_c, kb, 128), jnp.float32),
            pltpu.VMEM((rows, cols), jnp.float32),
            pltpu.VMEM((rows, 128), jnp.float32),
            dma((n_p, nch)), dma((n_p, nch)), dma((n_p, nch)),
            dma((n_p, n_c, nch)), dma((n_p, n_c, nch)), dma((n_c, nch)),
            dma((n_p,)), dma((n_p,)),
            dma((n_p, n_r)), dma((n_p, n_r)),
            dma((n_c,)), dma((n_c,)),
        ],
        compiler_params=pltpu.CompilerParams(
            collective_id=0, has_side_effects=True, vmem_limit_bytes=held + 6 * 2**20
        ),
    )(*operands)
    factor = jnp.float32(wide * n_c)
    return (factor * density.astype(jnp.float32)).astype(jnp.bfloat16)


def solution(mesh):
    return jax.shard_map(
        shards,
        mesh=mesh,
        in_specs=(
            P("rep", "row", "col"),
            P("rep", "row", "col"),
            P("rep", "row", "col"),
            P("rep", "row", "col"),
            P("row", ("col", "rep")),
        ),
        out_specs=P("row", ("col", "rep")),
        check_vma=False,
    )
```

```python
import functools

import jax
import jax.numpy as jnp
from jax import lax
from jax.experimental import pallas as pl
from jax.experimental.pallas import tpu as pltpu
from jax.sharding import PartitionSpec as P

MESH = pl.DeviceIdType.MESH


def kernel(
    n_r, n_c, n_p, nch,
    af_in, bf_in, of_in, a_in, b_in, out,
    af, bf, of, a, b, loads, abuf, bm, bsl, bbuf, dego, degr, acc, dacc,
    zr, zsl, zsr, xr, xs, ts, bzr, bzs, byr, bys, dr, ds,
):
    r, c, p = lax.axis_index("row"), lax.axis_index("col"), lax.axis_index("rep")
    rows, ka = a.shape
    kb = b.shape[0]
    width = rows // af.shape[1]
    cols = out.shape[1]
    ch_rows = rows // nch
    last = n_p - 1
    turns = n_p >= 4
    is_end = (p == 0) | (p == last)
    inner = 1 + lax.div(p, n_p // 2) * (last - 2)

    barrier = pltpu.get_barrier_semaphore()
    for axis, mine, count in (("row", r, n_r), ("col", c, n_c), ("rep", p, n_p)):
        for o in range(1, count):
            pl.semaphore_signal(
                barrier, inc=1, device_id={axis: lax.rem(mine + o, count)}, device_id_type=MESH
            )

    copies = [
        pltpu.make_async_copy(src, dst, loads.at[k])
        for k, (src, dst) in enumerate(
            ((af_in, af), (a_in, a), (bf_in, bf), (b_in, b), (of_in, of)))
    ]
    for copy in copies:
        copy.start()

    for copy in copies[:2]:
        copy.wait()

    for i in range(af.shape[1]):
        ch, off = divmod(i * width, ch_rows)
        for j in range(af.shape[0]):
            tile = a[i * width:(i + 1) * width, j * width:(j + 1) * width].astype(jnp.float32)
            abuf[p, c, ch, off:off + width, j * width:(j + 1) * width] = (
                tile * af[j, i].astype(jnp.float32)
            ).astype(jnp.bfloat16)

    pl.semaphore_wait(barrier, n_r + n_c + n_p - 3)

    def deg_copy(cc):
        return pltpu.make_async_remote_copy(
            src_ref=dego, dst_ref=degr.at[c], send_sem=ds.at[cc], recv_sem=dr.at[c],
            device_id={"col": cc}, device_id_type=MESH)

    def z_copy(g, ch, to, send):
        block = abuf.at[g, c, ch]
        return pltpu.make_async_remote_copy(
            src_ref=block, dst_ref=block, send_sem=send.at[g, ch], recv_sem=zr.at[g, ch],
            device_id={"rep": to}, device_id_type=MESH)

    def x_copy(g, ch, cc):
        block = abuf.at[g, c, ch]
        return pltpu.make_async_remote_copy(
            src_ref=block, dst_ref=block, send_sem=xs.at[g, cc, ch], recv_sem=xr.at[g, c, ch],
            device_id={"col": cc}, device_id_type=MESH)

    def bz_copy(pp):
        return pltpu.make_async_remote_copy(
            src_ref=bsl.at[pp], dst_ref=bbuf.at[p, pl.ds(pl.multiple_of(r * kb, kb), kb)],
            send_sem=bzs.at[pp], recv_sem=bzr.at[p], device_id={"rep": pp}, device_id_type=MESH)

    def by_copy(g, rr):
        block = bbuf.at[g, pl.ds(pl.multiple_of(r * kb, kb), kb)]
        return pltpu.make_async_remote_copy(
            src_ref=block, dst_ref=block, send_sem=bys.at[g, rr], recv_sem=byr.at[g, r],
            device_id={"row": rr}, device_id_type=MESH)

    def arrived(ref, sem):
        pltpu.make_async_copy(ref, ref, sem).wait()

    def others(mine, count, f):
        @pl.loop(1, count)
        def _(o):
            f(lax.rem(mine + o, count))

    def crosses(g):
        if not turns:
            return g >= 0
        return ((p != 1) | (g != 0)) & ((p != last - 1) | (g != last))

    def forward(g, ch):
        @pl.when(crosses(g))
        def _():
            others(c, n_c, lambda cc: x_copy(g, ch, cc).start())

    def turn_copy(cc, ch):
        block = abuf.at[p, cc, ch]
        return pltpu.make_async_remote_copy(
            src_ref=block, dst_ref=block, send_sem=ts.at[cc, ch], recv_sem=xr.at[p, cc, ch],
            device_id={"rep": inner}, device_id_type=MESH)

    def turn(ch):
        def one(cc):
            arrived(abuf.at[p, cc, ch], xr.at[p, cc, ch])
            turn_copy(cc, ch).start()

        @pl.when(is_end)
        def _():
            others(c, n_c, one)

    @pl.loop(0, nch)
    def _(ch):
        @pl.when(p > 0)
        def _():
            z_copy(p, ch, p - 1, zsl).start()

        @pl.when(p < n_p - 1)
        def _():
            z_copy(p, ch, p + 1, zsr).start()

    for copy in copies[2:]:
        copy.wait()

    for i in range(bf.shape[0]):
        for j in range(bf.shape[1]):
            at = (slice(i * width, (i + 1) * width), slice(j * width, (j + 1) * width))
            bm[at] = (b[at].astype(jnp.float32) * bf[i, j].astype(jnp.float32)).astype(jnp.bfloat16)
    dego[...] = jnp.dot(
        bm[...], jnp.ones((bm.shape[1], 128), jnp.bfloat16), preferred_element_type=jnp.float32
    )
    others(c, n_c, lambda cc: deg_copy(cc).start())

    @pl.when(is_end if turns else p >= 0)
    def _():
        @pl.loop(0, nch)
        def _(ch):
            forward(p, ch)

    def add_deg(cc):
        arrived(degr.at[cc], dr.at[cc])
        dego_sum[...] += degr[cc]

    dego_sum = dacc.at[pl.ds(0, kb)]
    dego_sum[...] = 1.0 + dego[...]
    others(c, n_c, add_deg)
    for t in range(bm.shape[1] // 128):
        pp, off = divmod(t * 128, cols)
        bsl[pp, :, off:off + 128] = (
            bm[:, t * 128:(t + 1) * 128].astype(jnp.float32) / dego_sum[...]
        ).astype(jnp.bfloat16)
    others(p, n_p, lambda pp: bz_copy(pp).start())
    bbuf[p, pl.ds(pl.multiple_of(r * kb, kb), kb)] = bsl[p]
    others(r, n_r, lambda rr: by_copy(p, rr).start())

    acc[...] = jnp.zeros_like(acc)
    dacc[...] = jnp.ones_like(dacc)

    def by_side(d, f):
        @pl.when(p >= d)
        def _():
            f(p - d)

        if d:
            @pl.when(p + d < n_p)
            def _():
                f(p + d)

    def block(g, cc, ch):
        left = abuf[g, cc, ch]
        right = bbuf[g, pl.ds(pl.multiple_of(cc * ka, ka), ka)]
        at = pl.ds(pl.multiple_of(ch * ch_rows, ch_rows), ch_rows)
        acc[at] += jnp.dot(left, right, preferred_element_type=jnp.float32)
        dacc[at] += jnp.dot(
            left, jnp.ones((ka, 128), jnp.bfloat16), preferred_element_type=jnp.float32
        )

    def own(d, ch):
        def one(g):
            @pl.when(ch == 0)
            def _():
                others(r, n_r, lambda rr: arrived(
                    bbuf.at[g, pl.ds(pl.multiple_of(rr * kb, kb), kb)], byr.at[g, rr]))

            block(g, c, ch)

        by_side(d, one)

    def crossed(d, ch):
        def one(g):
            def from_col(cc):
                @pl.when((g != p) | ~is_end if turns else g >= 0)
                def _():
                    arrived(abuf.at[g, cc, ch], xr.at[g, cc, ch])

                block(g, cc, ch)

            others(c, n_c, from_col)

        by_side(d, one)

    def pass_b(g):
        arrived(bbuf.at[g, pl.ds(pl.multiple_of(r * kb, kb), kb)], bzr.at[g])
        others(r, n_r, lambda rr: by_copy(g, rr).start())

    def finish(i):
        at = pl.ds(pl.multiple_of(i * width, width), width)
        scale = 1.0 / dacc[at]
        for j in range(of.shape[0]):
            tile = slice(j * width, (j + 1) * width)
            out[at, tile] = (
                acc[at, tile] * (scale * of[j, i].astype(jnp.float32))
            ).astype(jnp.bfloat16)

    for d in range(1, n_p + 1):
        if 1 < d < n_p:
            by_side(d, pass_b)

        @pl.loop(0, nch)
        def _(ch):
            def pass_a(g):
                arrived(abuf.at[g, c, ch], zr.at[g, ch])

                @pl.when((g < p) & (p < n_p - 1))
                def _():
                    z_copy(g, ch, p + 1, zsr).start()

                @pl.when((g > p) & (p > 0))
                def _():
                    z_copy(g, ch, p - 1, zsl).start()

                forward(g, ch)

            if d < n_p:
                by_side(d, pass_a)
            if d == 1:
                if turns:
                    turn(ch)

                    @pl.when(~is_end)
                    def _():
                        forward(p, ch)

                own(0, ch)
            if d == 2:
                own(1, ch)
                crossed(0, ch)
            if 1 < d <= n_p:
                crossed(d - 1, ch)
            if 1 < d < n_p:
                own(d, ch)
            if d == n_p:
                for i in range(ch_rows // width):
                    finish(ch * (ch_rows // width) + i)

        if d == 1:
            by_side(1, pass_b)

    if turns:
        @pl.when(is_end)
        def _():
            @pl.loop(0, nch)
            def _(ch):
                others(c, n_c, lambda cc: turn_copy(cc, ch).wait_send())

    others(c, n_c, lambda cc: deg_copy(cc).wait_send())
    others(p, n_p, lambda pp: bz_copy(pp).wait_send())

    @pl.loop(0, n_p)
    def _(g):
        others(r, n_r, lambda rr: by_copy(g, rr).wait_send())

        @pl.loop(0, nch)
        def _(ch):
            @pl.when(crosses(g))
            def _():
                others(c, n_c, lambda cc: x_copy(g, ch, cc).wait_send())

            @pl.when((g >= p) & (p > 0))
            def _():
                z_copy(g, ch, p - 1, zsl).wait_send()

            @pl.when((g <= p) & (p < n_p - 1))
            def _():
                z_copy(g, ch, p + 1, zsr).wait_send()


def shards(a_weights, a_flags, b_weights, b_flags, out_flags):
    n_r, n_c, n_p = (lax.axis_size(axis) for axis in ("row", "col", "rep"))
    _, rows, ka = a_weights.shape
    _, kb, wide = b_weights.shape
    cols = wide // n_p
    nch = max(1, 8 // n_c)
    dma = pltpu.SemaphoreType.DMA
    operands = (a_flags[0].T, b_flags[0], out_flags.T, a_weights[0], b_weights[0])
    density = pl.pallas_call(
        functools.partial(kernel, n_r, n_c, n_p, nch),
        out_shape=jax.ShapeDtypeStruct((rows, cols), jnp.bfloat16),
        in_specs=[pl.BlockSpec(memory_space=pl.ANY)] * 5,
        out_specs=pl.BlockSpec(memory_space=pltpu.VMEM),
        scratch_shapes=[
            *(pltpu.SMEM(x.shape, x.dtype) for x in operands[:3]),
            *(pltpu.VMEM(x.shape, x.dtype) for x in operands[3:]),
            dma((5,)),
            pltpu.VMEM((n_p, n_c, nch, rows // nch, ka), jnp.bfloat16),
            pltpu.VMEM((kb, wide), jnp.bfloat16),
            pltpu.VMEM((n_p, kb, cols), jnp.bfloat16),
            pltpu.VMEM((n_p, n_r * kb, cols), jnp.bfloat16),
            pltpu.VMEM((kb, 128), jnp.float32),
            pltpu.VMEM((n_c, kb, 128), jnp.float32),
            pltpu.VMEM((rows, cols), jnp.float32),
            pltpu.VMEM((rows, 128), jnp.float32),
            dma((n_p, nch)), dma((n_p, nch)), dma((n_p, nch)),
            dma((n_p, n_c, nch)), dma((n_p, n_c, nch)), dma((n_c, nch)),
            dma((n_p,)), dma((n_p,)),
            dma((n_p, n_r)), dma((n_p, n_r)),
            dma((n_c,)), dma((n_c,)),
        ],
        compiler_params=pltpu.CompilerParams(
            collective_id=0, has_side_effects=True, vmem_limit_bytes=56 * 2**20
        ),
    )(*operands)
    factor = jnp.float32(wide * n_c)
    return (factor * density.astype(jnp.float32)).astype(jnp.bfloat16)


def solution(mesh):
    return jax.shard_map(
        shards,
        mesh=mesh,
        in_specs=(
            P("rep", "row", "col"),
            P("rep", "row", "col"),
            P("rep", "row", "col"),
            P("rep", "row", "col"),
            P("row", ("col", "rep")),
        ),
        out_specs=P("row", ("col", "rep")),
        check_vma=False,
    )
```
